128 devices in a mesh: dp: 16 (over y_lo, z, core), seq: 8 (over x, y_hi).
Axes of the slice: x: 4, y: 4 (y_hi: 2, y_lo: 2; y = y_hi * 2 + y_lo), z: 4, core: 2. Of those that a mesh axis runs over, the one named last changes fastest.
Arguments:
- tokens: int32 [16, 131072], P('dp', 'seq'), may hold values from 0 to 4
- stem_weight: bfloat16 [60, 768], replicated, may hold values from -1.5 to 1.5
- stem_bias: float32 [768], replicated, may hold values from -3 to 3
- conv_gain: float32 [768], replicated, may hold values from 0.1 to 1.9
- conv_weight: bfloat16 [5, 768, 1536], P(None, 'dp'), may hold values from -0.09375 to 0.09375
- conv_bias: float32 [1536], replicated, may hold values from -3 to 3
- attn_gain: float32 [1536], replicated, may hold values from 0.1 to 1.9
- w_query: bfloat16 [1536, 1024], P('dp'), may hold values from -7 to 7
- w_key: bfloat16 [1536, 128], P('dp'), may hold values from -0.15625 to 0.15625
- w_value: bfloat16 [1536, 192], P('dp'), may hold values from -0.15625 to 0.15625
- w_out: bfloat16 [1536, 1536], P('dp'), may hold values from -0.4375 to 0.4375
Outputs:
- features: bfloat16 [16, 1024, 1536], P('dp', 'seq')
The draws below stay inside these ranges and needn't reach their ends.
Inputs may be any that keep to these rules, and one draw needn't show every extreme that they name: `tokens`: 0 is an unknown base; 1 to 4 are A, C, G, T.
All inputs are finite; a program needn't handle non-finite values.
Results may differ from the reference program's by a relative error of at most 0.009.
The reference program's roundings to bfloat16 on the way count: a program that leaves them out, or rounds other values in their place, can miss the bound.
Values may be sent and summed in bfloat16 or wider, within the bound.
No kernel may reach another device: no remote copies, remote signals or barrier semaphores. Data moves between devices by JAX's collectives and lax.ppermute only.
A program may use at most 192 MiB of HBM per device.

```python
import math
import jax
import jax.numpy as jnp
from jax import lax

D_STEM = 768
D = 1536
HEADS = 8
HEAD_K = 128
HEAD_V = 192
KW_STEM = 15
KW = 5
POOL_A = 8
POOL_B = 16
STEM_IN = 60
LENGTH = 131072
POSITIONS = 1024
WINDOWS = 16


def draw_w_query(key, part):
    normal_part = jnp.clip(jax.random.normal(key, (D, HEADS * HEAD_K), jnp.float32), -4.0, 4.0) * (1.0 / math.sqrt(D))
    return normal_part.astype(jnp.bfloat16)


def with_ends(drawn, rng, smallest, largest):
    extent = drawn.shape
    spot = [jax.random.randint(jax.random.fold_in(rng, axis), (), 0, extent[axis]) for axis in range(len(extent))]
    drawn = drawn.at[tuple(spot)].set(smallest)
    longest = extent.index(max(extent))
    spot[longest] = (spot[longest] + 1) % extent[longest]
    return drawn.at[tuple(spot)].set(largest)


def level_of(key, extent, split, least, high):
    def one(dim, blocks):
        draws = jax.random.uniform(jax.random.fold_in(jax.random.fold_in(key, 6), dim), (blocks,), jnp.float32, least / len(split), high / len(split))
        return jnp.repeat(jnp.exp(draws), extent[dim] // blocks).reshape((-1,) + (1,) * (len(extent) - dim - 1))

    loudness = one(*split[0])
    for cut in split[1:]:
        loudness = loudness * one(*cut)
    return loudness


def normal_values(own_key, shape, spread, most, cuts=(), held_as=jnp.bfloat16):
    level = level_of(own_key, shape, cuts, -0.22, 0.18) if cuts else 1.0
    array = jax.random.normal(own_key, shape, jnp.float32) * spread * level
    return jnp.minimum(jnp.maximum(array, -most), most).astype(held_as)


def setup_inputs(seed: int = 0) -> dict:
    streams_of = jax.random.split(jax.random.key(seed), 12)
    tokens = with_ends(jax.random.randint(streams_of[0], (WINDOWS, LENGTH), 0, 5), jax.random.fold_in(streams_of[0], 1), 0, 4).astype(jnp.int32)
    stem_weight = normal_values(streams_of[1], (STEM_IN, D_STEM), KW_STEM ** -0.5, 1.5)
    stem_bias = normal_values(streams_of[2], (D_STEM,), 0.5, 3.0, (), jnp.float32)
    conv_gain = jnp.clip(1.0 + 0.18 * jax.random.normal(streams_of[3], (D_STEM,), jnp.float32), 0.1, 1.9)
    conv_weight = normal_values(streams_of[4], (KW, D_STEM, D), (KW * D_STEM) ** -0.5, 0.09375, ((1, 16),))
    conv_bias = normal_values(streams_of[5], (D,), 0.5, 3.0, (), jnp.float32)
    attn_gain = jnp.clip(1.0 + 0.18 * jax.random.normal(streams_of[6], (D,), jnp.float32), 0.1, 1.9)
    w_query = draw_w_query(jax.random.fold_in(streams_of[11], 71), 0)
    w_key = normal_values(streams_of[8], (D, HEAD_K), D ** -0.5, 0.15625, ((0, 16),))
    w_value = normal_values(streams_of[9], (D, HEAD_V), D ** -0.5, 0.15625, ((0, 16),))
    w_out = normal_values(streams_of[10], (HEADS * HEAD_V, D), HEAD_V ** -0.5, 0.4375, ((0, 16),))
    return {"tokens": tokens, "stem_weight": stem_weight, "stem_bias": stem_bias, "conv_gain": conv_gain, "conv_weight": conv_weight, "conv_bias": conv_bias, "attn_gain": attn_gain, "w_query": w_query, "w_key": w_key, "w_value": w_value, "w_out": w_out}


epsilon = 1e-06

def stem_pool(padded_tokens, count, stem_weight, stem_bias):
    columns = jnp.stack([padded_tokens[offset:offset + count] for offset in range(KW_STEM)], axis=1)
    codes = jnp.arange(1, 5, dtype=jnp.int32)
    onehot = (columns[:, :, None] == codes).astype(jnp.bfloat16).reshape(count, KW_STEM * 4)
    block_len = min(count, 1024)
    onehot = onehot.reshape(count // block_len, block_len, KW_STEM * 4)

    def one_block(inputs):
        stem_rows = jnp.dot(inputs, stem_weight, preferred_element_type=jnp.float32) + stem_bias
        return jax.nn.gelu(lax.optimization_barrier(jnp.max(stem_rows.reshape(block_len // POOL_A, POOL_A, -1), axis=1)))
    return lax.map(one_block, onehot).reshape(count // POOL_A, -1).astype(jnp.bfloat16)

def rms_scale(values, gain):
    return values * lax.rsqrt(lax.optimization_barrier(jnp.mean(values * values, axis=-1, keepdims=True)) + epsilon) * gain

def rotate(values, angles):
    half_dim = values.shape[-1] // 2
    first = values[..., :half_dim]
    second = values[..., half_dim:]
    cosine = jnp.cos(angles)
    sine = jnp.sin(angles)
    return jnp.concatenate([first * cosine - second * sine, second * cosine + first * sine], axis=-1)

def reference(tokens, stem_weight, stem_bias, conv_gain, conv_weight, conv_bias, attn_gain, w_query, w_key, w_value, w_out):
    reach = KW_STEM // 2
    edge_rows = KW // 2

    def one_window(window_tokens):
        padded_tokens = jnp.pad(window_tokens, (reach, reach))
        pooled = stem_pool(padded_tokens, LENGTH, stem_weight, stem_bias)
        normed = rms_scale(pooled.astype(jnp.float32), conv_gain).astype(jnp.bfloat16)
        row_count = LENGTH // POOL_A
        padded_rows = jnp.pad(normed, ((edge_rows, edge_rows), (0, 0)))
        conv_sum = jnp.zeros((row_count, D), jnp.float32) + conv_bias
        for offset in range(KW):
            conv_sum = conv_sum + jnp.dot(padded_rows[offset:offset + row_count], conv_weight[offset], preferred_element_type=jnp.float32)
        coarse = lax.optimization_barrier(jnp.max(jax.nn.gelu(conv_sum).reshape(row_count // POOL_B, POOL_B, D), axis=1)).astype(jnp.bfloat16)
        residual = coarse.astype(jnp.float32)
        hidden = rms_scale(residual, attn_gain).astype(jnp.bfloat16)
        query = jnp.dot(hidden, w_query, preferred_element_type=jnp.float32).reshape(POSITIONS, HEADS, HEAD_K)
        keys = jnp.dot(hidden, w_key, preferred_element_type=jnp.float32)
        values = jnp.dot(hidden, w_value, preferred_element_type=jnp.float32).astype(jnp.bfloat16)
        half_dim = HEAD_K // 2
        freqs = 10000.0 ** (-jnp.arange(half_dim, dtype=jnp.float32) / half_dim)
        angles = jnp.arange(POSITIONS, dtype=jnp.int32).astype(jnp.float32)[:, None] * freqs[None, :]
        query = rotate(query, angles[:, None, :]).astype(jnp.bfloat16)
        keys = rotate(keys, angles).astype(jnp.bfloat16)
        scores = jnp.einsum('rhd,kd->hrk', query.astype(jnp.float32), keys.astype(jnp.float32)) * HEAD_K ** (-0.5)
        weights = jax.nn.softmax(scores, axis=-1).astype(jnp.bfloat16)
        mixed = jnp.einsum('hrk,kd->rhd', weights.astype(jnp.float32), values.astype(jnp.float32)).astype(jnp.bfloat16)
        mixed = mixed.reshape(POSITIONS, HEADS * HEAD_V)
        return (residual + jnp.dot(mixed, w_out, preferred_element_type=jnp.float32)).astype(jnp.bfloat16)
    return lax.map(one_window, tokens)
```

```python
import functools

import jax
import jax.numpy as jnp
import numpy as np
from jax import lax
from jax.experimental import pallas as pl
from jax.experimental.pallas import tpu as pltpu
from jax.sharding import PartitionSpec as P

D_STEM = 768
D = 1536
HEADS = 8
HEAD_K = 128
HEAD_V = 192
KW_STEM = 15
KW = 5
POOL_A = 8
POOL_B = 16
SHARDS = 16
CONV_ROWS = D_STEM // SHARDS
PROJ_ROWS = D // SHARDS
OUT_AT = KW * CONV_ROWS
QKV_AT = OUT_AT + PROJ_ROWS
BLOCK_ROWS = QKV_AT + PROJ_ROWS
CHUNK = 256
ROWS = 128
HALO = 24
EPSILON = 1e-06
AXES = ("dp", "seq")
VMEM_LIMIT = 60 * 1024 * 1024


def device_of(x, y, z, core):
    x, y, z = x % 4, y % 4, z % 4
    return ((y % 2) * 8 + z * 2 + core) * 8 + (x * 2 + y // 2)


def received_from(source):
    pairs = []
    for x in range(4):
        for y in range(4):
            for z in range(4):
                for core in range(2):
                    pairs.append((device_of(*source(x, y, z, core)), device_of(x, y, z, core)))
    return sorted(pairs)


def side(core):
    return 1 - 2 * core


def turn(x, core):
    return 1 - 2 * ((x + core) % 2)


FROM_Y = received_from(lambda x, y, z, core: (x, y + side(core), z, core))
FROM_X = received_from(lambda x, y, z, core: (x + side(core), y, z, core))
FROM_Z = received_from(lambda x, y, z, core: (x, y, z + turn(x, core), core))
FROM_CORE = received_from(lambda x, y, z, core: (x, y, z, 1 - core))


def shard_order():
    orders = np.zeros((SHARDS, 8, SHARDS), np.int32)
    for dp in range(SHARDS):
        for seq in range(8):
            y_low, z, core, x = dp // 8, (dp // 2) % 4, dp % 2, seq // 2

            def names(c):
                turned = turn(x, c)

                def shard(other, dz):
                    return (y_low ^ other) * 8 + (z + dz) % 4 * 2 + c

                return dict(
                    own=shard(0, 0), y=shard(1, 0), za=shard(0, turned), zb=shard(0, -turned),
                    zz=shard(0, 2), yza=shard(1, turned), yzb=shard(1, -turned), yzz=shard(1, 2),
                )

            mine, other = names(core), names(1 - core)
            order = [mine["own"], other["own"], mine["y"], mine["za"], other["y"], other["za"]]
            order += [mine["zb"], mine["zz"], mine["yza"], other["zb"], other["zz"], other["yza"]]
            order += [mine["yzb"], mine["yzz"], other["yzb"], other["yzz"]]
            orders[dp, seq] = order
    return orders


ORDERS = shard_order()


def dot(a, b):
    return jnp.dot(a, b, preferred_element_type=jnp.float32)


def gelu(x):
    return jax.nn.gelu(x)


def stem_kernel(edges, tokens, taps, bias, gain, out, hits):
    held = tokens[...].astype(jnp.float32)
    before = pltpu.roll(held, 1, 0)
    after = pltpu.roll(held, held.shape[0] - 1, 0)
    wide = jnp.concatenate([before, held, after], axis=1).astype(jnp.bfloat16)
    width = wide.shape[1]
    for g in range(POOL_B):
        token = lax.broadcasted_iota(jnp.int32, (width, 128), 0)
        lane = lax.broadcasted_iota(jnp.int32, (width, 128), 1)
        pick = (token == 120 + 8 * g + lane // 4).astype(jnp.float32).astype(jnp.bfloat16)
        spread = dot(wide, pick)
        code = (lax.broadcasted_iota(jnp.int32, spread.shape, 1) % 4 + 1).astype(jnp.float32)
        hit = (spread == code).astype(jnp.float32)
        hits[g * ROWS : (g + 1) * ROWS] = hit[:ROWS].astype(jnp.bfloat16)
        if g == 0:
            row_0 = hit[ROWS : ROWS + 1]
        if g == 1:
            row_1 = hit[ROWS : ROWS + 1]
        if g == 14:
            row_2 = hit[-1:]
        if g == 15:
            row_3 = hit[-1:]
    tail = jnp.concatenate([row_0, row_1, row_2, row_3, jnp.zeros((12, 128), jnp.float32)], axis=0)
    hits[POOL_B * ROWS :] = tail.astype(jnp.bfloat16)

    def normed(rows):
        best = dot(rows, taps[0])
        for offset in range(1, POOL_A):
            best = jnp.maximum(best, dot(rows, taps[offset]))
        pooled = gelu(best + bias[...]).astype(jnp.bfloat16).astype(jnp.float32)
        scale = lax.rsqrt(jnp.mean(pooled * pooled, axis=-1, keepdims=True) + EPSILON)
        return pooled * scale * gain[...]

    edge = normed(hits[POOL_B * ROWS :])
    high = jnp.where(edges[1] == 1, 0.0, edge[0:2])
    low = jnp.where(edges[0] == 1, 0.0, edge[2:4])

    def one(g, _):
        start = pl.multiple_of(g * ROWS, ROWS)
        out[g + 2] = normed(hits[pl.ds(start, ROWS)]).astype(jnp.bfloat16)
        return 0

    lax.fori_loop(0, POOL_B, one, 0)
    row = lax.broadcasted_iota(jnp.int32, (ROWS, D_STEM), 0)
    for i in range(2):
        block = out[POOL_B + i].astype(jnp.float32)
        out[i] = jnp.where(row == 0, low[i : i + 1], pltpu.roll(block, 1, 0)).astype(jnp.bfloat16)
        block = out[2 + i].astype(jnp.float32)
        block = jnp.where(row == ROWS - 1, high[i : i + 1], pltpu.roll(block, ROWS - 1, 0))
        out[POOL_B + 2 + i] = block.astype(jnp.bfloat16)


def stem(edges, tokens, taps, bias, gain):
    return pl.pallas_call(
        stem_kernel,
        out_shape=jax.ShapeDtypeStruct((POOL_B + 4, ROWS, D_STEM), jnp.bfloat16),
        in_specs=[pl.BlockSpec(memory_space=pltpu.SMEM)]
        + [pl.BlockSpec(memory_space=pltpu.VMEM)] * 4,
        out_specs=pl.BlockSpec(memory_space=pltpu.VMEM),
        scratch_shapes=[pltpu.VMEM((POOL_B * ROWS + 16, 128), jnp.bfloat16)],
        compiler_params=pltpu.CompilerParams(vmem_limit_bytes=VMEM_LIMIT),
        cost_estimate=pl.CostEstimate(flops=7_000_000_000, bytes_accessed=5_000_000, transcendentals=1_600_000),
        name="stem",
    )(edges, tokens, taps, bias, gain)


def pieces_of(part):
    pieces = []
    at = part * CHUNK
    while at < (part + 1) * CHUNK:
        block, row = divmod(at, CONV_ROWS)
        rows = min(CONV_ROWS - row, (part + 1) * CHUNK - at)
        pieces.append((block, row, rows, at - part * CHUNK))
        at += rows
    return pieces


STEP_G = 4


def conv_kernel(part, count, rows, *refs):
    blocks = refs[:count]
    acc_in = None
    at = count
    if part > 0:
        acc_in = refs[at]
        at += 1
    if part == 2:
        bias = refs[at]
        at += 1
    out = refs[at]
    weight, sems = refs[at + 1], refs[at + 2]
    pieces = pieces_of(part)
    first = pieces[0][0]
    step = pl.program_id(0)

    def copies(tap):
        return [
            pltpu.make_async_copy(
                blocks[block - first].at[pl.ds(tap * CONV_ROWS + row, size)],
                weight.at[tap, pl.ds(to, size)],
                sems.at[tap * len(pieces) + i],
            )
            for i, (block, row, size, to) in enumerate(pieces)
        ]

    @pl.when(step == 0)
    def _():
        for tap in range(KW):
            for copy in copies(tap):
                copy.start()
        for tap in range(KW):
            for copy in copies(tap):
                copy.wait()

    base = step * STEP_G
    columns = 512
    for n in range(D // columns):
        here = slice(n * columns, (n + 1) * columns)
        total = None
        for tap in range(KW):
            lhs = rows[pl.ds(base + tap, STEP_G)].reshape(STEP_G * ROWS, CHUNK)
            term = dot(lhs, weight[tap, :, here])
            total = term if total is None else total + term
        if part > 0:
            total = total + acc_in[:, here]
        if part < 2:
            out[:, here] = total
        else:
            total = total.reshape(STEP_G, ROWS, columns)
            most, least = jnp.max(total, axis=0), jnp.min(total, axis=0)
            most_ref, least_ref = refs[at + 3], refs[at + 4]

            @pl.when(step == 0)
            def _():
                most_ref[:, here] = most
                least_ref[:, here] = least

            @pl.when(step > 0)
            def _():
                most_ref[:, here] = jnp.maximum(most_ref[:, here], most)
                least_ref[:, here] = jnp.minimum(least_ref[:, here], least)

            @pl.when(step == POOL_B // STEP_G - 1)
            def _():
                shift = bias[:, here]
                coarse = jnp.maximum(gelu(most_ref[:, here] + shift), gelu(least_ref[:, here] + shift))
                out[:, here] = coarse.astype(jnp.bfloat16)


def conv_part(part, rows, blocks, acc=None, bias=None):
    pieces = pieces_of(part)
    blocks = blocks[pieces[0][0] : pieces[-1][0] + 1]
    step_rows = STEP_G * ROWS
    args = [rows, *blocks]
    in_specs = [pl.BlockSpec((POOL_B + 4, ROWS, CHUNK), lambda i, part=part: (0, 0, part))]
    in_specs += [pl.BlockSpec(memory_space=pl.ANY)] * len(blocks)
    acc_spec = pl.BlockSpec((step_rows, D), lambda i: (i, 0))
    scratch = [
        pltpu.VMEM((KW, CHUNK, D), jnp.bfloat16),
        pltpu.SemaphoreType.DMA((KW * len(pieces),)),
    ]
    if part > 0:
        args.append(acc)
        in_specs.append(acc_spec)
    if part == 2:
        args.append(bias)
        in_specs.append(pl.BlockSpec((1, D), lambda i: (0, 0)))
        out_shape = jax.ShapeDtypeStruct((ROWS, D), jnp.bfloat16)
        out_spec = pl.BlockSpec((ROWS, D), lambda i: (0, 0))
        scratch += [pltpu.VMEM((ROWS, D), jnp.float32)] * 2
    else:
        out_shape = jax.ShapeDtypeStruct((POOL_B * ROWS, D), jnp.float32)
        out_spec = acc_spec
    return pl.pallas_call(
        functools.partial(conv_kernel, part, len(blocks)),
        grid=(POOL_B // STEP_G,),
        out_shape=out_shape,
        in_specs=in_specs,
        out_specs=out_spec,
        scratch_shapes=scratch,
        compiler_params=pltpu.CompilerParams(vmem_limit_bytes=VMEM_LIMIT),
        cost_estimate=pl.CostEstimate(flops=8_053_063_680, bytes_accessed=20_000_000, transcendentals=0),
        name="conv",
    )(*args)


def turned(values, cosine, sine):
    return values * cosine + pltpu.roll(values, HEAD_K // 2, 1) * sine


def load_rows(order, blocks, row, column, width, target, sems):
    copies = [
        pltpu.make_async_copy(
            block.at[pl.ds(row, PROJ_ROWS), pl.ds(column, width)],
            target.at[pl.ds(pl.multiple_of(order[i] * PROJ_ROWS, PROJ_ROWS), PROJ_ROWS)],
            sems.at[i],
        )
        for i, block in enumerate(blocks)
    ]
    for copy in copies:
        copy.start()
    return copies


KV_WIDTH = 384


def keys_kernel(order, coarse, gain, cosine, sine, *refs):
    blocks = refs[:SHARDS]
    hidden, pair, weight, sems = refs[SHARDS:]
    copies = load_rows(order, blocks, QKV_AT, HEADS * HEAD_K, KV_WIDTH, weight, sems)
    residual = coarse[...].astype(jnp.float32)
    scale = lax.rsqrt(jnp.mean(residual * residual, axis=-1, keepdims=True) + EPSILON)
    rows = (residual * scale * gain[...]).astype(jnp.bfloat16)
    hidden[...] = rows
    for copy in copies:
        copy.wait()
    both = dot(rows, weight[...])
    pair[:, :HEAD_K] = turned(both[:, :HEAD_K], cosine[...], sine[...]).astype(jnp.bfloat16)
    pair[:, HEAD_K:] = both[:, HEAD_K:].astype(jnp.bfloat16)


def keys_of(order, coarse, gain, cosine, sine, blocks):
    vmem = pl.BlockSpec(memory_space=pltpu.VMEM)
    return pl.pallas_call(
        keys_kernel,
        out_shape=(
            jax.ShapeDtypeStruct((ROWS, D), jnp.bfloat16),
            jax.ShapeDtypeStruct((ROWS, KV_WIDTH), jnp.bfloat16),
        ),
        in_specs=[pl.BlockSpec(memory_space=pltpu.SMEM)] + [vmem] * 4 + [pl.BlockSpec(memory_space=pl.ANY)] * SHARDS,
        out_specs=(vmem, vmem),
        scratch_shapes=[pltpu.VMEM((D, KV_WIDTH), jnp.bfloat16), pltpu.SemaphoreType.DMA((SHARDS,))],
        compiler_params=pltpu.CompilerParams(vmem_limit_bytes=VMEM_LIMIT),
        cost_estimate=pl.CostEstimate(flops=150_000_000, bytes_accessed=2_000_000, transcendentals=0),
        name="keys",
    )(order, coarse, gain, cosine, sine, *blocks)


def query_kernel(order, hidden, cosine, sine, *refs):
    blocks = refs[:SHARDS]
    out, weight, sems = refs[SHARDS:]
    for copy in load_rows(order, blocks, QKV_AT, 0, HEADS * HEAD_K, weight, sems):
        copy.wait()
    for head in range(HEADS):
        query = dot(hidden[...], weight[:, head * HEAD_K : (head + 1) * HEAD_K])
        out[head] = turned(query, cosine[...], sine[...]).astype(jnp.bfloat16)


def query_of(order, hidden, cosine, sine, blocks):
    vmem = pl.BlockSpec(memory_space=pltpu.VMEM)
    return pl.pallas_call(
        query_kernel,
        out_shape=jax.ShapeDtypeStruct((HEADS, ROWS, HEAD_K), jnp.bfloat16),
        in_specs=[pl.BlockSpec(memory_space=pltpu.SMEM)] + [vmem] * 3 + [pl.BlockSpec(memory_space=pl.ANY)] * SHARDS,
        out_specs=vmem,
        scratch_shapes=[pltpu.VMEM((D, HEADS * HEAD_K), jnp.bfloat16), pltpu.SemaphoreType.DMA((SHARDS,))],
        compiler_params=pltpu.CompilerParams(vmem_limit_bytes=VMEM_LIMIT),
        cost_estimate=pl.CostEstimate(flops=1_600_000_000, bytes_accessed=4_000_000, transcendentals=0),
        name="query",
    )(order, hidden, cosine, sine, *blocks)


def attention_kernel(order, coarse, query, *refs):
    pairs, blocks = refs[:8], refs[8 : 8 + SHARDS]
    out, weight, sems = refs[8 + SHARDS :]
    copies = load_rows(order, blocks, OUT_AT, 0, D, weight, sems)
    keys = jnp.concatenate([pair[:, :HEAD_K] for pair in pairs], axis=0)
    values = jnp.concatenate([pair[:, HEAD_K:] for pair in pairs], axis=0)
    mixed = []
    for head in range(HEADS):
        scores = lax.dot_general(
            query[head], keys, (((1,), (1,)), ((), ())), preferred_element_type=jnp.float32
        ) * HEAD_K ** (-0.5)
        raised = jnp.exp(scores - jnp.max(scores, axis=-1, keepdims=True))
        weights = raised / jnp.sum(raised, axis=-1, keepdims=True)
        mixed.append(dot(weights.astype(jnp.bfloat16), values).astype(jnp.bfloat16)[:, :HEAD_V])
    for copy in copies:
        copy.wait()
    total = coarse[...].astype(jnp.float32)
    for head in range(HEADS):
        total = total + dot(mixed[head], weight[head * HEAD_V : (head + 1) * HEAD_V])
    out[...] = total.astype(jnp.bfloat16)


def attention(order, coarse, query, pairs, blocks):
    vmem = pl.BlockSpec(memory_space=pltpu.VMEM)
    return pl.pallas_call(
        attention_kernel,
        out_shape=jax.ShapeDtypeStruct((ROWS, D), jnp.bfloat16),
        in_specs=[pl.BlockSpec(memory_space=pltpu.SMEM)] + [vmem] * 10 + [pl.BlockSpec(memory_space=pl.ANY)] * SHARDS,
        out_specs=vmem,
        scratch_shapes=[pltpu.VMEM((D, D), jnp.bfloat16), pltpu.SemaphoreType.DMA((SHARDS,))],
        compiler_params=pltpu.CompilerParams(vmem_limit_bytes=VMEM_LIMIT),
        cost_estimate=pl.CostEstimate(flops=3_000_000_000, bytes_accessed=6_000_000, transcendentals=1_000_000),
        name="attention",
    )(order, coarse, query, *pairs, *blocks)


def move(value, pairs):
    return lax.ppermute(value, AXES, pairs)


def body(
    tokens,
    stem_weight,
    stem_bias,
    conv_gain,
    conv_weight,
    conv_bias,
    attn_gain,
    w_query,
    w_key,
    w_value,
    w_out,
):
    seq = lax.axis_index("seq")
    line = tokens[0]
    up = [(i, i + 1) for i in range(7)]
    down = [(i + 1, i) for i in range(7)]
    low = lax.ppermute(line[-HALO:], "seq", up)
    high = lax.ppermute(line[:HALO], "seq", down)

    projections = jnp.pad(
        jnp.concatenate([w_query, w_key, w_value], axis=1), ((0, 0), (0, D - HEADS * HEAD_K - HEAD_K - HEAD_V))
    )
    own = jnp.concatenate([conv_weight.reshape(OUT_AT, D), w_out, projections], axis=0)
    own_o = move(own, FROM_CORE)
    y = move(own, FROM_Y)
    za = move(own, FROM_Z)
    order = jnp.asarray(ORDERS)[lax.axis_index("dp"), seq]
    source = (order[:, None] * CONV_ROWS + jnp.arange(CONV_ROWS)[None, :]).reshape(1, D_STEM)
    chosen = jnp.arange(D_STEM)[:, None] == source
    weight = dot(stem_weight, chosen.astype(jnp.bfloat16)).astype(jnp.bfloat16)
    bias, gain = (
        jnp.sum(jnp.where(chosen, vector[:, None], 0.0), axis=0, keepdims=True)
        for vector in (stem_bias, conv_gain)
    )
    taps = jnp.stack([jnp.pad(weight, ((4 * (j + 1), 128 - 60 - 4 * (j + 1)), (0, 0))) for j in range(POOL_A)])
    half = HEAD_K // 2
    freqs = 10000.0 ** (-jnp.arange(half, dtype=jnp.float32) / half)
    positions = seq * ROWS + jnp.arange(ROWS, dtype=jnp.int32)
    angles = positions.astype(jnp.float32)[:, None] * freqs[None, :]
    cosine = jnp.tile(jnp.cos(angles), (1, 2))
    sine = jnp.sin(angles)
    sine = jnp.concatenate([-sine, sine], axis=1)

    rows = jnp.concatenate(
        [
            line.reshape(ROWS, 128),
            jnp.pad(high, (0, 128 - HALO))[None],
            jnp.zeros((14, 128), jnp.int32),
            jnp.pad(low, (128 - HALO, 0))[None],
        ],
        axis=0,
    )
    edges = jnp.stack([seq == 0, seq == 7]).astype(jnp.int32)
    normed = stem(edges, rows, taps, bias, gain)

    zb = move(za, FROM_X)
    yza = move(za, FROM_Y)
    zz = move(za, FROM_Z)
    y_o, za_o = move(y, FROM_CORE), move(za, FROM_CORE)
    blocks = [own, own_o, y, za, y_o, za_o]
    total = conv_part(0, normed, blocks)
    yzb = move(yza, FROM_X)
    yzz = move(zz, FROM_Y)
    blocks += [zb, zz, yza] + [move(b, FROM_CORE) for b in (zb, zz, yza)]
    total = conv_part(1, normed, blocks, total)
    blocks += [yzb, yzz, move(yzb, FROM_CORE), move(yzz, FROM_CORE)]
    coarse = conv_part(2, normed, blocks, total, conv_bias[None])

    hidden, pair = keys_of(order, coarse, attn_gain[None], cosine, sine, blocks)
    pairs = [pair] + [
        lax.ppermute(pair, "seq", [(i, (i + shift) % 8) for i in range(8)]) for shift in range(1, 8)
    ]
    query = query_of(order, hidden, cosine, sine, blocks)
    return attention(order, coarse, query, pairs, blocks)[None]


def solution(mesh):
    in_specs = (
        P("dp", "seq"),
        P(),
        P(),
        P(),
        P(None, "dp", None),
        P(),
        P(),
        P("dp", None),
        P("dp", None),
        P("dp", None),
        P("dp", None),
    )
    out_specs = P("dp", "seq", None)
    return jax.shard_map(body, mesh=mesh, in_specs=in_specs, out_specs=out_specs, check_vma=False)
```

```python
import functools

import jax
import jax.numpy as jnp
import numpy as np
from jax import lax
from jax.experimental import pallas as pl
from jax.experimental.pallas import tpu as pltpu
from jax.sharding import PartitionSpec as P

D_STEM = 768
D = 1536
HEADS = 8
HEAD_K = 128
HEAD_V = 192
KW_STEM = 15
KW = 5
POOL_A = 8
POOL_B = 16
SHARDS = 16
CONV_ROWS = D_STEM // SHARDS
PROJ_ROWS = D // SHARDS
OUT_AT = KW * CONV_ROWS
QKV_AT = OUT_AT + PROJ_ROWS
BLOCK_ROWS = QKV_AT + PROJ_ROWS
CHUNK = 256
ROWS = 128
HALO = 24
EPSILON = 1e-06
AXES = ("dp", "seq")
VMEM_LIMIT = 60 * 1024 * 1024


def device_of(x, y, z, core):
    x, y, z = x % 4, y % 4, z % 4
    return ((y % 2) * 8 + z * 2 + core) * 8 + (x * 2 + y // 2)


def received_from(source):
    pairs = []
    for x in range(4):
        for y in range(4):
            for z in range(4):
                for core in range(2):
                    pairs.append((device_of(*source(x, y, z, core)), device_of(x, y, z, core)))
    return sorted(pairs)


def side(core):
    return 1 - 2 * core


def turn(x, core):
    return 1 - 2 * ((x + core) % 2)


FROM_Y = received_from(lambda x, y, z, core: (x, y + side(core), z, core))
FROM_X = received_from(lambda x, y, z, core: (x + side(core), y, z, core))
FROM_Z = received_from(lambda x, y, z, core: (x, y, z + turn(x, core), core))
FROM_CORE = received_from(lambda x, y, z, core: (x, y, z, 1 - core))


def shard_order():
    orders = np.zeros((SHARDS, 8, SHARDS), np.int32)
    for dp in range(SHARDS):
        for seq in range(8):
            y_low, z, core, x = dp // 8, (dp // 2) % 4, dp % 2, seq // 2

            def names(c):
                turned = turn(x, c)

                def shard(other, dz):
                    return (y_low ^ other) * 8 + (z + dz) % 4 * 2 + c

                return dict(
                    own=shard(0, 0), y=shard(1, 0), za=shard(0, turned), zb=shard(0, -turned),
                    zz=shard(0, 2), yza=shard(1, turned), yzb=shard(1, -turned), yzz=shard(1, 2),
                )

            mine, other = names(core), names(1 - core)
            order = [mine["own"], other["own"], mine["y"], mine["za"], other["y"], other["za"]]
            order += [mine["zb"], mine["zz"], mine["yza"], other["zb"], other["zz"], other["yza"]]
            order += [mine["yzb"], mine["yzz"], other["yzb"], other["yzz"]]
            orders[dp, seq] = order
    return orders


def trig():
    half = HEAD_K // 2
    freqs = np.float32(10000.0) ** (-np.arange(half, dtype=np.float32) / np.float32(half))
    angles = np.arange(8 * ROWS, dtype=np.float32)[:, None] * freqs[None, :]
    cosine, sine = np.cos(angles.astype(np.float64)), np.sin(angles.astype(np.float64))
    table = [np.concatenate([cosine, cosine], axis=1), np.concatenate([-sine, sine], axis=1)]
    return np.stack([t.reshape(8, ROWS, HEAD_K) for t in table], axis=1).astype(np.float32)


PLACES = np.concatenate(
    [shard_order(), np.broadcast_to(np.arange(8, dtype=np.int32)[None, :, None], (SHARDS, 8, 1))], axis=2
)
ANGLES = trig()


def dot(a, b):
    return jnp.dot(a, b, preferred_element_type=jnp.float32)


def gelu(x):
    return jax.nn.gelu(x)


STEM_ROWS = 512
FULL = POOL_B * ROWS


def hits_of(wide, g):
    width = wide.shape[1]
    token = lax.broadcasted_iota(jnp.int32, (width, 128), 0)
    lane = lax.broadcasted_iota(jnp.int32, (width, 128), 1)
    pick = (token == 120 + 8 * g + lane // 4).astype(jnp.float32).astype(jnp.bfloat16)
    spread = dot(wide, pick)
    code = (lax.broadcasted_iota(jnp.int32, spread.shape, 1) % 4 + 1).astype(jnp.float32)
    return (spread == code).astype(jnp.float32)


def strongest(rows, taps, columns):
    most = dot(rows, taps[0:128, columns])
    for offset in range(1, POOL_A):
        most = jnp.maximum(most, dot(rows, taps[offset * 128 : (offset + 1) * 128, columns]))
    return most


def stem_norm(most, bias, gain):
    pooled = gelu(most + bias).astype(jnp.bfloat16).astype(jnp.float32)
    scale = lax.rsqrt(jnp.mean(pooled * pooled, axis=-1, keepdims=True) + EPSILON)
    return pooled * scale * gain


def stem_kernel(order, tokens, weight, bias, gain, out, taps, vectors, hits, best):
    lane = lax.broadcasted_iota(jnp.int32, (D_STEM, D_STEM), 1)
    source = lax.broadcasted_iota(jnp.int32, (1, D_STEM), 1)
    for i in range(SHARDS):
        here = lax.broadcasted_iota(jnp.int32, (1, D_STEM), 1)
        source = jnp.where(here >= i * CONV_ROWS, here + (order[i] - i) * CONV_ROWS, source)
    channel = lax.broadcasted_iota(jnp.int32, (D_STEM, D_STEM), 0)
    chosen = (channel == source).astype(jnp.float32).astype(jnp.bfloat16)
    parts = []
    for vector in (bias[...], gain[...]):
        for _ in range(3):
            parts.append(vector.astype(jnp.bfloat16).astype(jnp.float32))
            vector = vector - parts[-1]
    parts = jnp.concatenate(parts + [jnp.zeros((10, D_STEM), jnp.float32)], axis=0)
    parts = dot(parts.astype(jnp.bfloat16), chosen)
    vectors[0:1] = parts[0:1] + parts[1:2] + parts[2:3]
    vectors[1:2] = parts[3:4] + parts[4:5] + parts[5:6]
    vectors[2:] = jnp.zeros((6, D_STEM), jnp.float32)
    moved = dot(weight[...], chosen).astype(jnp.bfloat16)
    row = lax.broadcasted_iota(jnp.int32, (POOL_A * 128, 4 * KW_STEM), 0)
    tap = lax.broadcasted_iota(jnp.int32, (POOL_A * 128, 4 * KW_STEM), 1)
    place = (row % 128 == tap + 4 * (row // 128 + 1)).astype(jnp.float32).astype(jnp.bfloat16)
    taps[...] = dot(place, moved).astype(jnp.bfloat16)

    held = tokens[...].astype(jnp.float32)
    before, after = pltpu.roll(held, 1, 0), pltpu.roll(held, ROWS - 1, 0)
    wide = jnp.concatenate([before, held, after], axis=1).astype(jnp.bfloat16)
    for g in range(POOL_B):
        hits[g * ROWS : (g + 1) * ROWS] = hits_of(wide, g).astype(jnp.bfloat16)

    def one(i, _):
        rows = hits[pl.ds(pl.multiple_of(i * STEM_ROWS, STEM_ROWS), STEM_ROWS)]
        for n in range(D_STEM // 256):
            here = slice(n * 256, (n + 1) * 256)
            best[:, here] = strongest(rows, taps, here)
        for k in range(STEM_ROWS // ROWS):
            block = stem_norm(best[k * ROWS : (k + 1) * ROWS], vectors[0:1], vectors[1:2])
            out[i * (STEM_ROWS // ROWS) + k + 2] = block.astype(jnp.bfloat16)
        return 0

    lax.fori_loop(0, FULL // STEM_ROWS, one, 0)
    for i in range(2):
        block = out[POOL_B + i].astype(jnp.float32)
        out[i] = pltpu.roll(block, 1, 0).astype(jnp.bfloat16)
        block = out[2 + i].astype(jnp.float32)
        out[POOL_B + 2 + i] = pltpu.roll(block, ROWS - 1, 0).astype(jnp.bfloat16)


def stem(order, tokens, weight, bias, gain):
    vmem = pl.BlockSpec(memory_space=pltpu.VMEM)
    return pl.pallas_call(
        stem_kernel,
        out_shape=(
            jax.ShapeDtypeStruct((POOL_B + 4, ROWS, D_STEM), jnp.bfloat16),
            jax.ShapeDtypeStruct((POOL_A * 128, D_STEM), jnp.bfloat16),
            jax.ShapeDtypeStruct((8, D_STEM), jnp.float32),
        ),
        in_specs=[pl.BlockSpec(memory_space=pltpu.SMEM)] + [vmem] * 4,
        out_specs=(vmem, vmem, vmem),
        scratch_shapes=[
            pltpu.VMEM((FULL, 128), jnp.bfloat16),
            pltpu.VMEM((STEM_ROWS, D_STEM), jnp.float32),
        ],
        compiler_params=pltpu.CompilerParams(vmem_limit_bytes=VMEM_LIMIT),
        cost_estimate=pl.CostEstimate(flops=7_000_000_000, bytes_accessed=5_000_000, transcendentals=1_600_000),
        name="stem",
    )(order, tokens, weight, bias, gain)


def edge_kernel(order, tokens, low_row, high_row, taps, vectors, out):
    at_start = order[SHARDS] == 0
    at_end = order[SHARDS] == 7
    low = jnp.where(at_start, 0, low_row[...])
    high = jnp.where(at_end, 0, high_row[...])
    first, last = tokens[0:1], tokens[ROWS - 1 : ROWS]
    lines = [(low, low, first), (low, first, first), (last, last, high), (last, high, high)]
    wide = jnp.concatenate([jnp.concatenate(line, axis=1) for line in lines] + [jnp.zeros((12, 384), jnp.int32)], axis=0)
    wide = wide.astype(jnp.float32).astype(jnp.bfloat16)
    by_row = {g: hits_of(wide, g) for g in (0, 1, 14, 15)}
    wanted = [(14, 0), (15, 0), (0, 1), (15, 2), (0, 3), (1, 3)]
    rows = [by_row[g][line : line + 1] for g, line in wanted] + [jnp.zeros((10, 128), jnp.float32)]
    rows = jnp.concatenate(rows, axis=0).astype(jnp.bfloat16)
    normed = stem_norm(strongest(rows, taps, slice(0, D_STEM)), vectors[0:1], vectors[1:2])
    row = lax.broadcasted_iota(jnp.int32, normed.shape, 0)
    outside = ((row < 2) & at_start) | ((row > 3) & at_end)
    out[...] = jnp.where(outside, 0.0, normed)


def edges(order, tokens, low, high, taps, vectors):
    vmem = pl.BlockSpec(memory_space=pltpu.VMEM)
    return pl.pallas_call(
        edge_kernel,
        out_shape=jax.ShapeDtypeStruct((16, D_STEM), jnp.float32),
        in_specs=[pl.BlockSpec(memory_space=pltpu.SMEM)] + [vmem] * 5,
        out_specs=vmem,
        compiler_params=pltpu.CompilerParams(vmem_limit_bytes=VMEM_LIMIT),
        cost_estimate=pl.CostEstimate(flops=30_000_000, bytes_accessed=2_000_000, transcendentals=10_000),
        name="edges",
    )(order, tokens, low, high, taps, vectors)


def pack_kernel(conv, w_out, w_query, w_key, w_value, out):
    for tap in range(KW):
        out[tap * CONV_ROWS : (tap + 1) * CONV_ROWS] = conv[tap]
    out[OUT_AT:QKV_AT] = w_out[...]
    at = 0
    for piece in (w_query, w_key, w_value):
        width = piece.shape[1]
        out[QKV_AT:, at : at + width] = piece[...]
        at += width
    out[QKV_AT:, at:] = jnp.zeros((PROJ_ROWS, D - at), jnp.bfloat16)


def pack(*pieces):
    vmem = pl.BlockSpec(memory_space=pltpu.VMEM)
    return pl.pallas_call(
        pack_kernel,
        out_shape=jax.ShapeDtypeStruct((BLOCK_ROWS, D), jnp.bfloat16),
        in_specs=[vmem] * 5,
        out_specs=vmem,
        compiler_params=pltpu.CompilerParams(vmem_limit_bytes=VMEM_LIMIT),
        name="pack",
    )(*pieces)


def pieces_of(part):
    pieces = []
    at = part * CHUNK
    while at < (part + 1) * CHUNK:
        block, row = divmod(at, CONV_ROWS)
        rows = min(CONV_ROWS - row, (part + 1) * CHUNK - at)
        pieces.append((block, row, rows, at - part * CHUNK))
        at += rows
    return pieces


COLUMNS = 512
PAIRS = 4
KV_WIDTH = 384


def conv_kernel(part, count, order, rows, patch, *refs):
    blocks, refs = refs[:count], refs[count:]
    if part > 0:
        acc_in, refs = refs[0], refs[1:]
    if part == 2:
        bias, gain, angles = refs[:3]
        coarse, pair, query = refs[3:6]
        refs = refs[6:]
    else:
        out, refs = refs[0], refs[1:]
    held, lhs_a, lhs_b, lhs_c, lhs_d, w_a, w_b, w_c, w_d, w_1, sems, held_sem = refs[:12]
    if part == 2:
        most_ref, least_ref, weight, weight_sems = refs[12:]
    pieces = pieces_of(part)
    first = pieces[0][0]
    third, step = pl.program_id(0), pl.program_id(1)
    homes = [(w_a, 0), (w_1, 0), (w_d, 0), (w_a, CHUNK), (w_d, CHUNK)]

    def copies(n):
        here = pl.ds(n * COLUMNS, COLUMNS)
        return [
            pltpu.make_async_copy(
                blocks[block - first].at[pl.ds(tap * CONV_ROWS + row, size), here],
                homes[tap][0].at[n, pl.ds(homes[tap][1] + to, size)],
                sems.at[(n * KW + tap) * len(pieces) + i],
            )
            for tap in range(KW)
            for i, (block, row, size, to) in enumerate(pieces)
        ]

    def projection_copies():
        return [
            pltpu.make_async_copy(
                block.at[pl.ds(QKV_AT, PROJ_ROWS), pl.ds(0, D - 128)],
                weight.at[pl.ds(pl.multiple_of(order[(first + i) % SHARDS] * PROJ_ROWS, PROJ_ROWS), PROJ_ROWS)],
                weight_sems.at[i],
            )
            for i, block in enumerate(blocks)
        ]

    @pl.when((third == 0) & (step == 0))
    def _():
        load = pltpu.make_async_copy(rows.at[:, :, pl.ds(part * CHUNK, CHUNK)], held, held_sem)
        load.start()
        for n in range(D // COLUMNS):
            for copy in copies(n):
                copy.start()
        if part == 2:
            for copy in projection_copies():
                copy.start()
        load.wait()
        row = lax.broadcasted_iota(jnp.int32, (16, CHUNK), 0)
        edge = patch[...]
        for i, block in enumerate((0, 1, 2, POOL_B + 1, POOL_B + 2, POOL_B + 3)):
            at, which = (0, 0) if i < 3 else (ROWS - 16, 15)
            old = held[block, at : at + 16].astype(jnp.float32)
            held[block, at : at + 16] = jnp.where(row == which, edge[i : i + 1], old).astype(jnp.bfloat16)
        for m in range(POOL_B // 2):
            even, odd = [held[2 * m + 2 * k] for k in range(3)], [held[2 * m + 2 * k + 1] for k in range(3)]
            lhs_a[m, :, :CHUNK] = even[0] - even[1]
            lhs_a[m, :, CHUNK:] = odd[1] - even[2]
            lhs_b[m, :, :CHUNK] = odd[0] + even[1]
            lhs_b[m, :, CHUNK:] = even[2]
            lhs_c[m] = even[1] - odd[0]
            lhs_d[m, :, :CHUNK] = odd[0] - odd[1]
            lhs_d[m, :, CHUNK:] = even[2] - odd[2]

    @pl.when(step == 0)
    def _():
        for n in range(D // COLUMNS):

            @pl.when(third == n)
            def _():
                for copy in copies(n):
                    copy.wait()

        outer = (w_a[third, :CHUNK].astype(jnp.float32) + w_d[third, :CHUNK].astype(jnp.float32)) * 0.5
        inner = w_1[third].astype(jnp.float32) * 0.5
        w_b[:CHUNK] = (outer + inner).astype(jnp.bfloat16)
        w_c[...] = (outer - inner).astype(jnp.bfloat16)
        w_b[CHUNK:] = w_a[third, CHUNK:] + w_d[third, CHUNK:]

    def part_of(lhs):
        return lhs[pl.ds(step * PAIRS, PAIRS)].reshape(PAIRS * ROWS, -1)

    a = dot(part_of(lhs_a), w_a[third])
    b = dot(part_of(lhs_b), w_b[...])
    c = dot(part_of(lhs_c), w_c[...])
    d = dot(part_of(lhs_d), w_d[third])
    even = (a + (b + c)).reshape(PAIRS, ROWS, COLUMNS)
    odd = ((b - c) - d).reshape(PAIRS, ROWS, COLUMNS)
    if part > 0:
        even = even + acc_in[0]
        odd = odd + acc_in[1]
    if part < 2:
        out[0] = even
        out[1] = odd
        return
    most = jnp.max(jnp.maximum(even, odd), axis=0)
    least = jnp.min(jnp.minimum(even, odd), axis=0)

    @pl.when(step == 0)
    def _():
        most_ref[...] = most
        least_ref[...] = least

    last = POOL_B // 2 // PAIRS - 1
    for n in range(D // COLUMNS):

        @pl.when((step == last) & (third == n))
        def _():
            here = slice(n * COLUMNS, (n + 1) * COLUMNS)
            shift = bias[:, here]
            high = jnp.maximum(most_ref[...], most) + shift
            low = jnp.minimum(least_ref[...], least) + shift
            coarse[:, here] = jnp.maximum(gelu(high), gelu(low)).astype(jnp.bfloat16)

    @pl.when((step == last) & (third == D // COLUMNS - 1))
    def _():
        residual = coarse[...].astype(jnp.float32)
        scale = lax.rsqrt(jnp.mean(residual * residual, axis=-1, keepdims=True) + EPSILON)
        hidden = (residual * scale * gain[...]).astype(jnp.bfloat16)
        for copy in projection_copies():
            copy.wait()
        made = dot(hidden, weight[...])
        cosine, sine = angles[0], angles[1]
        for head in range(HEADS):
            one = made[:, head * HEAD_K : (head + 1) * HEAD_K]
            query[head * ROWS : (head + 1) * ROWS] = turned(one, cosine, sine).astype(jnp.bfloat16)
        at = HEADS * HEAD_K
        pair[:, :HEAD_K] = turned(made[:, at : at + HEAD_K], cosine, sine).astype(jnp.bfloat16)
        pair[:, HEAD_K:] = made[:, at + HEAD_K : at + KV_WIDTH].astype(jnp.bfloat16)


def conv_part(part, order, rows, patch, blocks, acc=None, rest=()):
    pieces = pieces_of(part)
    if part < 2:
        blocks = blocks[pieces[0][0] : pieces[-1][0] + 1]
        used = blocks
    else:
        used = blocks[pieces[0][0] :] + blocks[: pieces[0][0]]
    args = [order, rows, patch, *used]
    whole = pl.BlockSpec(memory_space=pltpu.VMEM)
    in_specs = [
        pl.BlockSpec(memory_space=pltpu.SMEM),
        pl.BlockSpec(memory_space=pl.ANY),
        pl.BlockSpec((16, CHUNK), lambda i, j, part=part: (0, part)),
    ]
    in_specs += [pl.BlockSpec(memory_space=pl.ANY)] * len(used)
    acc_shape = (2, POOL_B // 2, ROWS, D)
    acc_spec = pl.BlockSpec((2, PAIRS, ROWS, COLUMNS), lambda i, j: (0, j, 0, i))
    lhs = (POOL_B // 2, ROWS)
    thirds = D // COLUMNS
    scratch = [
        pltpu.VMEM((POOL_B + 4, ROWS, CHUNK), jnp.bfloat16),
        pltpu.VMEM((*lhs, 2 * CHUNK), jnp.bfloat16),
        pltpu.VMEM((*lhs, 2 * CHUNK), jnp.bfloat16),
        pltpu.VMEM((*lhs, CHUNK), jnp.bfloat16),
        pltpu.VMEM((*lhs, 2 * CHUNK), jnp.bfloat16),
        pltpu.VMEM((thirds, 2 * CHUNK, COLUMNS), jnp.bfloat16),
        pltpu.VMEM((2 * CHUNK, COLUMNS), jnp.bfloat16),
        pltpu.VMEM((CHUNK, COLUMNS), jnp.bfloat16),
        pltpu.VMEM((thirds, 2 * CHUNK, COLUMNS), jnp.bfloat16),
        pltpu.VMEM((thirds, CHUNK, COLUMNS), jnp.bfloat16),
        pltpu.SemaphoreType.DMA((thirds * KW * len(pieces),)),
        pltpu.SemaphoreType.DMA,
    ]
    if part > 0:
        args.append(acc)
        in_specs.append(acc_spec)
    if part == 2:
        args += rest
        in_specs += [whole] * 3
        out_shape = (
            jax.ShapeDtypeStruct((ROWS, D), jnp.bfloat16),
            jax.ShapeDtypeStruct((ROWS, KV_WIDTH), jnp.bfloat16),
            jax.ShapeDtypeStruct((HEADS * ROWS, HEAD_K), jnp.bfloat16),
        )
        out_spec = (whole, whole, whole)
        scratch += [pltpu.VMEM((ROWS, COLUMNS), jnp.float32)] * 2
        scratch += [pltpu.VMEM((D, D - 128), jnp.bfloat16), pltpu.SemaphoreType.DMA((SHARDS,))]
    else:
        out_shape = jax.ShapeDtypeStruct(acc_shape, jnp.float32)
        out_spec = acc_spec
    return pl.pallas_call(
        functools.partial(conv_kernel, part, len(used)),
        grid=(thirds, POOL_B // 2 // PAIRS),
        out_shape=out_shape,
        in_specs=in_specs,
        out_specs=out_spec,
        scratch_shapes=scratch,
        compiler_params=pltpu.CompilerParams(vmem_limit_bytes=VMEM_LIMIT),
        cost_estimate=pl.CostEstimate(flops=8_053_063_680, bytes_accessed=20_000_000, transcendentals=0),
        name="conv",
    )(*args)


def turned(values, cosine, sine):
    return values * cosine + pltpu.roll(values, HEAD_K // 2, 1) * sine


def load_rows(order, blocks, row, column, width, target, sems):
    copies = [
        pltpu.make_async_copy(
            block.at[pl.ds(row, PROJ_ROWS), pl.ds(column, width)],
            target.at[pl.ds(pl.multiple_of(order[i] * PROJ_ROWS, PROJ_ROWS), PROJ_ROWS)],
            sems.at[i],
        )
        for i, block in enumerate(blocks)
    ]
    for copy in copies:
        copy.start()
    return copies


def attention_kernel(order, coarse, *refs):
    queries, pairs, blocks = refs[0], refs[1:5], refs[5 : 5 + SHARDS]
    out, weight, sems = refs[5 + SHARDS :]
    copies = load_rows(order, blocks, OUT_AT, 0, D, weight, sems)
    keys = jnp.concatenate([pair[:, :HEAD_K] for pair in pairs], axis=0)
    values = jnp.concatenate([pair[:, HEAD_K:] for pair in pairs], axis=0)
    mixed = []
    for head in range(HEADS):
        query = queries[head * ROWS : (head + 1) * ROWS]
        scores = lax.dot_general(query, keys, (((1,), (1,)), ((), ())), preferred_element_type=jnp.float32)
        scores = scores * HEAD_K ** (-0.5)
        raised = jnp.exp(scores - jnp.max(scores, axis=-1, keepdims=True))
        weights = raised * (1.0 / jnp.sum(raised, axis=-1, keepdims=True))
        mixed.append(dot(weights.astype(jnp.bfloat16), values).astype(jnp.bfloat16)[:, :HEAD_V])
    for copy in copies:
        copy.wait()
    total = coarse[...].astype(jnp.float32)
    for head in range(HEADS):
        total = total + dot(mixed[head], weight[head * HEAD_V : (head + 1) * HEAD_V])
    out[...] = total.astype(jnp.bfloat16)


def attention(order, coarse, query, pairs, blocks):
    vmem = pl.BlockSpec(memory_space=pltpu.VMEM)
    return pl.pallas_call(
        attention_kernel,
        out_shape=jax.ShapeDtypeStruct((ROWS, D), jnp.bfloat16),
        in_specs=[pl.BlockSpec(memory_space=pltpu.SMEM)] + [vmem] * 6 + [pl.BlockSpec(memory_space=pl.ANY)] * SHARDS,
        out_specs=vmem,
        scratch_shapes=[pltpu.VMEM((D, D), jnp.bfloat16), pltpu.SemaphoreType.DMA((SHARDS,))],
        compiler_params=pltpu.CompilerParams(vmem_limit_bytes=VMEM_LIMIT),
        cost_estimate=pl.CostEstimate(flops=3_000_000_000, bytes_accessed=6_000_000, transcendentals=1_000_000),
        name="attention",
    )(order, coarse, query, *pairs, *blocks)


def move(value, pairs):
    return lax.ppermute(value, AXES, pairs)


def body(
    tokens,
    stem_weight,
    stem_bias,
    conv_gain,
    conv_weight,
    conv_bias,
    attn_gain,
    w_query,
    w_key,
    w_value,
    w_out,
):
    seq = lax.axis_index("seq")
    line = tokens.reshape(ROWS, 128)
    own = pack(conv_weight, w_out, w_query, w_key, w_value)
    own_o = move(own, FROM_CORE)
    y = move(own, FROM_Y)
    za = move(own, FROM_Z)
    low = lax.ppermute(line[-1:], "seq", [(i, (i + 1) % 8) for i in range(8)])
    high = lax.ppermute(line[:1], "seq", [(i, (i - 1) % 8) for i in range(8)])
    order = jnp.asarray(PLACES)[lax.axis_index("dp"), seq]
    normed, taps, vectors = stem(order, line, stem_weight, stem_bias[None], conv_gain[None])
    y, za, own_o, low, high, normed = lax.optimization_barrier((y, za, own_o, low, high, normed))

    y_o, za_o = move(y, FROM_CORE), move(za, FROM_CORE)
    zb = move(za, FROM_X)
    yza = move(za, FROM_Y)
    zz = move(za, FROM_Z)
    patch = edges(order, line, low, high, taps, vectors)
    blocks = [own, own_o, y, za, y_o, za_o]
    total = conv_part(0, order, normed, patch, blocks)
    zb, yza, zz, total = lax.optimization_barrier((zb, yza, zz, total))
    yzb = move(yza, FROM_X)
    yzz = move(zz, FROM_Y)
    blocks += [zb, zz, yza] + [move(b, FROM_CORE) for b in (zb, zz, yza)]
    total = conv_part(1, order, normed, patch, blocks, total)
    yzb, yzz, total = lax.optimization_barrier((yzb, yzz, total))
    blocks += [yzb, yzz, move(yzb, FROM_CORE), move(yzz, FROM_CORE)]
    angles = jnp.asarray(ANGLES)[seq]
    rest = (conv_bias[None], attn_gain[None], angles)
    coarse, pair, query = conv_part(2, order, normed, patch, blocks, total, rest)

    near = lax.ppermute(pair, "seq", [(i, i ^ 1) for i in range(8)])
    both = jnp.concatenate([pair, near], axis=0)
    pairs = [both] + [
        lax.ppermute(both, "seq", [(i, (i + shift) % 8) for i in range(8)]) for shift in (2, 6, 4)
    ]
    return attention(order, coarse, query, pairs, blocks)[None]


def solution(mesh):
    in_specs = (
        P("dp", "seq"),
        P(),
        P(),
        P(),
        P(None, "dp", None),
        P(),
        P(),
        P("dp", None),
        P("dp", None),
        P("dp", None),
        P("dp", None),
    )
    out_specs = P("dp", "seq", None)
    return jax.shard_map(body, mesh=mesh, in_specs=in_specs, out_specs=out_specs, check_vma=False)
```

```python
import functools

import jax
import jax.numpy as jnp
import numpy as np
from jax import lax
from jax.experimental import pallas as pl
from jax.experimental.pallas import tpu as pltpu
from jax.sharding import PartitionSpec as P

D_STEM = 768
D = 1536
HEADS = 8
HEAD_K = 128
HEAD_V = 192
KW_STEM = 15
KW = 5
POOL_A = 8
POOL_B = 16
SHARDS = 16
CONV_ROWS = D_STEM // SHARDS
PROJ_ROWS = D // SHARDS
OUT_AT = KW * CONV_ROWS
QKV_AT = OUT_AT + PROJ_ROWS
BLOCK_ROWS = QKV_AT + PROJ_ROWS
ROWS = 128
HALO = 24
EPSILON = 1e-06
AXES = ("dp", "seq")
VMEM_LIMIT = 60 * 1024 * 1024


def device_of(x, y, z, core):
    x, y, z = x % 4, y % 4, z % 4
    return ((y % 2) * 8 + z * 2 + core) * 8 + (x * 2 + y // 2)


def received_from(source):
    pairs = []
    for x in range(4):
        for y in range(4):
            for z in range(4):
                for core in range(2):
                    pairs.append((device_of(*source(x, y, z, core)), device_of(x, y, z, core)))
    return sorted(pairs)


def side(core):
    return 1 - 2 * core


def turn(x, core):
    return 1 - 2 * ((x + core) % 2)


FROM_Y = received_from(lambda x, y, z, core: (x, y + side(core), z, core))
FROM_X = received_from(lambda x, y, z, core: (x + side(core), y, z, core))
FROM_Z = received_from(lambda x, y, z, core: (x, y, z + turn(x, core), core))
FROM_CORE = received_from(lambda x, y, z, core: (x, y, z, 1 - core))


def shard_order():
    orders = np.zeros((SHARDS, 8, SHARDS), np.int32)
    for dp in range(SHARDS):
        for seq in range(8):
            y_low, z, core, x = dp // 8, (dp // 2) % 4, dp % 2, seq // 2

            def names(c):
                turned = turn(x, c)

                def shard(other, dz):
                    return (y_low ^ other) * 8 + (z + dz) % 4 * 2 + c

                return dict(
                    own=shard(0, 0), y=shard(1, 0), za=shard(0, turned), zb=shard(0, -turned),
                    zz=shard(0, 2), yza=shard(1, turned), yzb=shard(1, -turned), yzz=shard(1, 2),
                )

            mine, other = names(core), names(1 - core)
            order = [mine["own"], other["own"], mine["y"], mine["za"], other["y"], other["za"]]
            order += [mine["zb"], mine["zz"], mine["yza"], other["zb"], other["zz"], other["yza"]]
            order += [mine["yzb"], mine["yzz"], other["yzb"], other["yzz"]]
            orders[dp, seq] = order
    return orders


def trig():
    half = HEAD_K // 2
    freqs = np.float32(10000.0) ** (-np.arange(half, dtype=np.float32) / np.float32(half))
    angles = np.arange(8 * ROWS, dtype=np.float32)[:, None] * freqs[None, :]
    cosine, sine = np.cos(angles.astype(np.float64)), np.sin(angles.astype(np.float64))
    table = [np.concatenate([cosine, cosine], axis=1), np.concatenate([-sine, sine], axis=1)]
    return np.stack([t.reshape(8, ROWS, HEAD_K) for t in table], axis=1).astype(np.float32)


PLACES = np.concatenate(
    [shard_order(), np.broadcast_to(np.arange(8, dtype=np.int32)[None, :, None], (SHARDS, 8, 1))], axis=2
)
ANGLES = trig()


def dot(a, b):
    return jnp.dot(a, b, preferred_element_type=jnp.float32)


def gelu(x):
    return jax.nn.gelu(x)


STEM_ROWS = 512
FULL = POOL_B * ROWS


def hits_of(wide, g):
    width = wide.shape[1]
    token = lax.broadcasted_iota(jnp.int32, (width, 128), 0)
    lane = lax.broadcasted_iota(jnp.int32, (width, 128), 1)
    pick = (token == 120 + 8 * g + lane // 4).astype(jnp.float32).astype(jnp.bfloat16)
    spread = dot(wide, pick)
    code = (lax.broadcasted_iota(jnp.int32, spread.shape, 1) % 4 + 1).astype(jnp.float32)
    return (spread == code).astype(jnp.float32)


def strongest(rows, taps, columns):
    most = dot(rows, taps[0:128, columns])
    for offset in range(1, POOL_A):
        most = jnp.maximum(most, dot(rows, taps[offset * 128 : (offset + 1) * 128, columns]))
    return most


def stem_norm(most, bias, gain):
    pooled = gelu(most + bias).astype(jnp.bfloat16).astype(jnp.float32)
    scale = lax.rsqrt(jnp.mean(pooled * pooled, axis=-1, keepdims=True) + EPSILON)
    return pooled * scale * gain


def stem_kernel(order, tokens, weight, bias, gain, out, taps, vectors, hits, best):
    lane = lax.broadcasted_iota(jnp.int32, (D_STEM, D_STEM), 1)
    source = lax.broadcasted_iota(jnp.int32, (1, D_STEM), 1)
    for i in range(SHARDS):
        here = lax.broadcasted_iota(jnp.int32, (1, D_STEM), 1)
        source = jnp.where(here >= i * CONV_ROWS, here + (order[i] - i) * CONV_ROWS, source)
    channel = lax.broadcasted_iota(jnp.int32, (D_STEM, D_STEM), 0)
    chosen = (channel == source).astype(jnp.float32).astype(jnp.bfloat16)
    parts = []
    for vector in (bias[...], gain[...]):
        for _ in range(3):
            parts.append(vector.astype(jnp.bfloat16).astype(jnp.float32))
            vector = vector - parts[-1]
    parts = jnp.concatenate(parts + [jnp.zeros((10, D_STEM), jnp.float32)], axis=0)
    parts = dot(parts.astype(jnp.bfloat16), chosen)
    vectors[0:1] = parts[0:1] + parts[1:2] + parts[2:3]
    vectors[1:2] = parts[3:4] + parts[4:5] + parts[5:6]
    vectors[2:] = jnp.zeros((6, D_STEM), jnp.float32)
    moved = dot(weight[...], chosen).astype(jnp.bfloat16)
    row = lax.broadcasted_iota(jnp.int32, (POOL_A * 128, 4 * KW_STEM), 0)
    tap = lax.broadcasted_iota(jnp.int32, (POOL_A * 128, 4 * KW_STEM), 1)
    place = (row % 128 == tap + 4 * (row // 128 + 1)).astype(jnp.float32).astype(jnp.bfloat16)
    taps[...] = dot(place, moved).astype(jnp.bfloat16)

    stem_rows(0, tokens, taps, vectors, out, hits, best)


def stem_rows(half, tokens, taps, vectors, out, hits, best):
    held = tokens[...].astype(jnp.float32)
    before, after = pltpu.roll(held, 1, 0), pltpu.roll(held, ROWS - 1, 0)
    wide = jnp.concatenate([before, held, after], axis=1).astype(jnp.bfloat16)
    for k in range(POOL_B // 2):
        hits[k * ROWS : (k + 1) * ROWS] = hits_of(wide, half * (POOL_B // 2) + k).astype(jnp.bfloat16)

    def one(i, _):
        rows = hits[pl.ds(pl.multiple_of(i * STEM_ROWS, STEM_ROWS), STEM_ROWS)]
        for n in range(D_STEM // 256):
            here = slice(n * 256, (n + 1) * 256)
            best[:, here] = strongest(rows, taps, here)
        for k in range(STEM_ROWS // ROWS):
            block = stem_norm(best[k * ROWS : (k + 1) * ROWS], vectors[0:1], vectors[1:2])
            out[i * (STEM_ROWS // ROWS) + k + 2 * half] = block.astype(jnp.bfloat16)
        return 0

    lax.fori_loop(0, FULL // 2 // STEM_ROWS, one, 0)
    for i in range(2):
        source, to, by = (i, 8 + i, ROWS - 1) if half == 0 else (8 + i, i, 1)
        out[to] = pltpu.roll(out[source].astype(jnp.float32), by, 0).astype(jnp.bfloat16)


def stem_front(order, tokens, weight, bias, gain):
    vmem = pl.BlockSpec(memory_space=pltpu.VMEM)
    return pl.pallas_call(
        stem_kernel,
        out_shape=(
            jax.ShapeDtypeStruct((POOL_B // 2 + 2, ROWS, D_STEM), jnp.bfloat16),
            jax.ShapeDtypeStruct((POOL_A * 128, D_STEM), jnp.bfloat16),
            jax.ShapeDtypeStruct((8, D_STEM), jnp.float32),
        ),
        in_specs=[pl.BlockSpec(memory_space=pltpu.SMEM)] + [vmem] * 4,
        out_specs=(vmem, vmem, vmem),
        scratch_shapes=[
            pltpu.VMEM((FULL // 2, 128), jnp.bfloat16),
            pltpu.VMEM((STEM_ROWS, D_STEM), jnp.float32),
        ],
        compiler_params=pltpu.CompilerParams(vmem_limit_bytes=VMEM_LIMIT),
        cost_estimate=pl.CostEstimate(flops=4_000_000_000, bytes_accessed=5_000_000, transcendentals=800_000),
        name="stem_front",
    )(order, tokens, weight, bias, gain)


def stem_back(tokens, taps, vectors):
    vmem = pl.BlockSpec(memory_space=pltpu.VMEM)
    return pl.pallas_call(
        functools.partial(stem_rows, 1),
        out_shape=jax.ShapeDtypeStruct((POOL_B // 2 + 2, ROWS, D_STEM), jnp.bfloat16),
        in_specs=[vmem] * 3,
        out_specs=vmem,
        scratch_shapes=[
            pltpu.VMEM((FULL // 2, 128), jnp.bfloat16),
            pltpu.VMEM((STEM_ROWS, D_STEM), jnp.float32),
        ],
        compiler_params=pltpu.CompilerParams(vmem_limit_bytes=VMEM_LIMIT),
        cost_estimate=pl.CostEstimate(flops=3_500_000_000, bytes_accessed=4_000_000, transcendentals=800_000),
        name="stem_back",
    )(tokens, taps, vectors)


def edge_kernel(order, tokens, low_row, high_row, taps, vectors, out):
    at_start = order[SHARDS] == 0
    at_end = order[SHARDS] == 7
    low = jnp.where(at_start, 0, low_row[...])
    high = jnp.where(at_end, 0, high_row[...])
    first, last = tokens[0:1], tokens[ROWS - 1 : ROWS]
    lines = [(low, low, first), (low, first, first), (last, last, high), (last, high, high)]
    wide = jnp.concatenate([jnp.concatenate(line, axis=1) for line in lines] + [jnp.zeros((12, 384), jnp.int32)], axis=0)
    wide = wide.astype(jnp.float32).astype(jnp.bfloat16)
    by_row = {g: hits_of(wide, g) for g in (0, 1, 14, 15)}
    wanted = [(14, 0), (15, 0), (0, 1), (15, 2), (0, 3), (1, 3)]
    rows = [by_row[g][line : line + 1] for g, line in wanted] + [jnp.zeros((10, 128), jnp.float32)]
    rows = jnp.concatenate(rows, axis=0).astype(jnp.bfloat16)
    normed = stem_norm(strongest(rows, taps, slice(0, D_STEM)), vectors[0:1], vectors[1:2])
    row = lax.broadcasted_iota(jnp.int32, normed.shape, 0)
    outside = ((row < 2) & at_start) | ((row > 3) & at_end)
    out[...] = jnp.where(outside, 0.0, normed)


def edges(order, tokens, low, high, taps, vectors):
    vmem = pl.BlockSpec(memory_space=pltpu.VMEM)
    return pl.pallas_call(
        edge_kernel,
        out_shape=jax.ShapeDtypeStruct((16, D_STEM), jnp.float32),
        in_specs=[pl.BlockSpec(memory_space=pltpu.SMEM)] + [vmem] * 5,
        out_specs=vmem,
        compiler_params=pltpu.CompilerParams(vmem_limit_bytes=VMEM_LIMIT),
        cost_estimate=pl.CostEstimate(flops=30_000_000, bytes_accessed=2_000_000, transcendentals=10_000),
        name="edges",
    )(order, tokens, low, high, taps, vectors)


def pack_kernel(conv, w_out, w_query, w_key, w_value, out):
    for tap in range(KW):
        out[tap * CONV_ROWS : (tap + 1) * CONV_ROWS] = conv[tap]
    out[OUT_AT:QKV_AT] = w_out[...]
    at = 0
    for piece in (w_query, w_key, w_value):
        width = piece.shape[1]
        out[QKV_AT:, at : at + width] = piece[...]
        at += width
    out[QKV_AT:, at:] = jnp.zeros((PROJ_ROWS, D - at), jnp.bfloat16)


def pack(*pieces):
    vmem = pl.BlockSpec(memory_space=pltpu.VMEM)
    return pl.pallas_call(
        pack_kernel,
        out_shape=jax.ShapeDtypeStruct((BLOCK_ROWS, D), jnp.bfloat16),
        in_specs=[vmem] * 5,
        out_specs=vmem,
        compiler_params=pltpu.CompilerParams(vmem_limit_bytes=VMEM_LIMIT),
        name="pack",
    )(*pieces)


PARTS = ((0, 512), (512, 256))


def pieces_of(part):
    start, size = PARTS[part]
    pieces = []
    at = start
    while at < start + size:
        block, row = divmod(at, CONV_ROWS)
        rows = min(CONV_ROWS - row, start + size - at)
        pieces.append((block, row, rows, at - start))
        at += rows
    return pieces


COLUMNS = 512
PAIRS = 4
KV_WIDTH = 384


def conv_kernel(part, count, order, front, back, patch, *refs):
    blocks, refs = refs[:count], refs[count:]
    if part == 1:
        acc_in, bias, gain, angles = refs[:4]
        coarse, hidden, pair = refs[4:7]
        refs = refs[7:]
    else:
        out, refs = refs[0], refs[1:]
    held, lhs_a, lhs_b, lhs_c, lhs_d, w_a, w_b, w_c, w_d, w_1, sems, held_sems = refs[:12]
    if part == 1:
        most_ref, least_ref, weight, weight_sems = refs[12:]
    pieces = pieces_of(part)
    first = pieces[0][0]
    start, size = PARTS[part]
    third, step = pl.program_id(0), pl.program_id(1)
    columns = pl.ds(pl.multiple_of(third * COLUMNS, COLUMNS), COLUMNS)
    homes = [(w_a, 0), (w_1, 0), (w_d, 0), (w_a, size), (w_d, size)]

    def copies():
        return [
            pltpu.make_async_copy(
                blocks[block - first].at[pl.ds(tap * CONV_ROWS + row, rows)],
                homes[tap][0].at[pl.ds(homes[tap][1] + to, rows)],
                sems.at[tap * len(pieces) + i],
            )
            for tap in range(KW)
            for i, (block, row, rows, to) in enumerate(pieces)
        ]

    def row_copies():
        return [
            pltpu.make_async_copy(
                source.at[pl.ds(at, rows), :, pl.ds(start, size)],
                held.at[pl.ds(to, rows)],
                held_sems.at[i],
            )
            for i, (source, at, rows, to) in enumerate(
                ((front, 0, 8, 2), (back, 0, 2, 0), (back, 2, 8, 10), (front, 8, 2, 18))
            )
        ]

    def projection_copies():
        return [
            pltpu.make_async_copy(
                block.at[pl.ds(QKV_AT, PROJ_ROWS), pl.ds(HEADS * HEAD_K, KV_WIDTH)],
                weight.at[pl.ds(pl.multiple_of(order[(first + i) % SHARDS] * PROJ_ROWS, PROJ_ROWS), PROJ_ROWS)],
                weight_sems.at[i],
            )
            for i, block in enumerate(blocks)
        ]

    @pl.when((third == 0) & (step == 0))
    def _():
        for copy in row_copies() + copies():
            copy.start()
        if part == 1:
            for copy in projection_copies():
                copy.start()
        for copy in row_copies():
            copy.wait()
        row = lax.broadcasted_iota(jnp.int32, (16, size), 0)
        edge = patch[...]
        for i, block in enumerate((0, 1, 2, POOL_B + 1, POOL_B + 2, POOL_B + 3)):
            at, which = (0, 0) if i < 3 else (ROWS - 16, 15)
            old = held[block, at : at + 16].astype(jnp.float32)
            held[block, at : at + 16] = jnp.where(row == which, edge[i : i + 1], old).astype(jnp.bfloat16)
        for m in range(POOL_B // 2):
            even, odd = [held[2 * m + 2 * k] for k in range(3)], [held[2 * m + 2 * k + 1] for k in range(3)]
            lhs_a[m, :, :size] = even[0] - even[1]
            lhs_a[m, :, size:] = odd[1] - even[2]
            lhs_b[m, :, :size] = odd[0] + even[1]
            lhs_b[m, :, size:] = even[2]
            lhs_c[m] = even[1] - odd[0]
            lhs_d[m, :, :size] = odd[0] - odd[1]
            lhs_d[m, :, size:] = even[2] - odd[2]
        for copy in copies():
            copy.wait()

    @pl.when(step == 0)
    def _():
        outer = (w_a[:size, columns].astype(jnp.float32) + w_d[:size, columns].astype(jnp.float32)) * 0.5
        inner = w_1[:, columns].astype(jnp.float32) * 0.5
        w_b[:size] = (outer + inner).astype(jnp.bfloat16)
        w_c[...] = (outer - inner).astype(jnp.bfloat16)
        w_b[size:] = w_a[size:, columns] + w_d[size:, columns]

    def part_of(lhs):
        return lhs[pl.ds(step * PAIRS, PAIRS)].reshape(PAIRS * ROWS, -1)

    a = dot(part_of(lhs_a), w_a[:, columns])
    b = dot(part_of(lhs_b), w_b[...])
    c = dot(part_of(lhs_c), w_c[...])
    d = dot(part_of(lhs_d), w_d[:, columns])
    even = (a + (b + c)).reshape(PAIRS, ROWS, COLUMNS)
    odd = ((b - c) - d).reshape(PAIRS, ROWS, COLUMNS)
    if part == 1:
        even = even + acc_in[0]
        odd = odd + acc_in[1]
    else:
        out[0] = even
        out[1] = odd
        return
    most = jnp.max(jnp.maximum(even, odd), axis=0)
    least = jnp.min(jnp.minimum(even, odd), axis=0)

    @pl.when(step == 0)
    def _():
        most_ref[...] = most
        least_ref[...] = least

    last = POOL_B // 2 // PAIRS - 1
    for n in range(D // COLUMNS):

        @pl.when((step == last) & (third == n))
        def _():
            here = slice(n * COLUMNS, (n + 1) * COLUMNS)
            shift = bias[:, here]
            high = jnp.maximum(most_ref[...], most) + shift
            low = jnp.minimum(least_ref[...], least) + shift
            coarse[:, here] = jnp.maximum(gelu(high), gelu(low)).astype(jnp.bfloat16)

    @pl.when((step == last) & (third == D // COLUMNS - 1))
    def _():
        residual = coarse[...].astype(jnp.float32)
        scale = lax.rsqrt(jnp.mean(residual * residual, axis=-1, keepdims=True) + EPSILON)
        hidden[...] = (residual * scale * gain[...]).astype(jnp.bfloat16)
        for copy in projection_copies():
            copy.wait()
        made = dot(hidden[...], weight[...])
        pair[:, :HEAD_K] = turned(made[:, :HEAD_K], angles[0], angles[1]).astype(jnp.bfloat16)
        pair[:, HEAD_K:] = made[:, HEAD_K:].astype(jnp.bfloat16)


def conv_part(part, order, front, back, patch, blocks, rest=()):
    pieces = pieces_of(part)
    start, size = PARTS[part]
    used = blocks[: pieces[-1][0] + 1] if part == 0 else blocks[pieces[0][0] :] + blocks[: pieces[0][0]]
    args = [order, front, back, patch, *used]
    whole = pl.BlockSpec(memory_space=pltpu.VMEM)
    in_specs = [
        pl.BlockSpec(memory_space=pltpu.SMEM),
        pl.BlockSpec(memory_space=pl.ANY),
        pl.BlockSpec(memory_space=pl.ANY),
        pl.BlockSpec((16, size), lambda i, j: (0, start // size)),
    ]
    in_specs += [pl.BlockSpec(memory_space=pl.ANY)] * len(used)
    acc_spec = pl.BlockSpec((2, PAIRS, ROWS, COLUMNS), lambda i, j: (0, j, 0, i))
    lhs = (POOL_B // 2, ROWS)
    scratch = [
        pltpu.VMEM((POOL_B + 4, ROWS, size), jnp.bfloat16),
        pltpu.VMEM((*lhs, 2 * size), jnp.bfloat16),
        pltpu.VMEM((*lhs, 2 * size), jnp.bfloat16),
        pltpu.VMEM((*lhs, size), jnp.bfloat16),
        pltpu.VMEM((*lhs, 2 * size), jnp.bfloat16),
        pltpu.VMEM((2 * size, D), jnp.bfloat16),
        pltpu.VMEM((2 * size, COLUMNS), jnp.bfloat16),
        pltpu.VMEM((size, COLUMNS), jnp.bfloat16),
        pltpu.VMEM((2 * size, D), jnp.bfloat16),
        pltpu.VMEM((size, D), jnp.bfloat16),
        pltpu.SemaphoreType.DMA((KW * len(pieces),)),
        pltpu.SemaphoreType.DMA((4,)),
    ]
    if part == 1:
        args += rest
        in_specs += [acc_spec] + [whole] * 3
        out_shape = (
            jax.ShapeDtypeStruct((ROWS, D), jnp.bfloat16),
            jax.ShapeDtypeStruct((ROWS, D), jnp.bfloat16),
            jax.ShapeDtypeStruct((ROWS, KV_WIDTH), jnp.bfloat16),
        )
        out_spec = (whole, whole, whole)
        scratch += [pltpu.VMEM((ROWS, COLUMNS), jnp.float32)] * 2
        scratch += [pltpu.VMEM((D, KV_WIDTH), jnp.bfloat16), pltpu.SemaphoreType.DMA((SHARDS,))]
    else:
        out_shape = jax.ShapeDtypeStruct((2, POOL_B // 2, ROWS, D), jnp.float32)
        out_spec = acc_spec
    return pl.pallas_call(
        functools.partial(conv_kernel, part, len(used)),
        grid=(D // COLUMNS, POOL_B // 2 // PAIRS),
        out_shape=out_shape,
        in_specs=in_specs,
        out_specs=out_spec,
        scratch_shapes=scratch,
        compiler_params=pltpu.CompilerParams(vmem_limit_bytes=VMEM_LIMIT),
        cost_estimate=pl.CostEstimate(flops=size * 22_020_096, bytes_accessed=20_000_000, transcendentals=0),
        name="conv",
    )(*args)


def turned(values, cosine, sine):
    return values * cosine + pltpu.roll(values, HEAD_K // 2, 1) * sine


def load_rows(order, blocks, row, column, width, target, sems):
    copies = [
        pltpu.make_async_copy(
            block.at[pl.ds(row, PROJ_ROWS), pl.ds(column, width)],
            target.at[pl.ds(pl.multiple_of(order[i] * PROJ_ROWS, PROJ_ROWS), PROJ_ROWS)],
            sems.at[i],
        )
        for i, block in enumerate(blocks)
    ]
    for copy in copies:
        copy.start()
    return copies


def query_kernel(order, hidden, angles, *refs):
    blocks = refs[:SHARDS]
    out, weight, sems = refs[SHARDS:]
    for copy in load_rows(order, blocks, QKV_AT, 0, HEADS * HEAD_K, weight, sems):
        copy.wait()
    query = dot(hidden[...], weight[...])
    for head in range(HEADS):
        one = query[:, head * HEAD_K : (head + 1) * HEAD_K]
        out[head * ROWS : (head + 1) * ROWS] = turned(one, angles[0], angles[1]).astype(jnp.bfloat16)


def query_of(order, hidden, angles, blocks):
    vmem = pl.BlockSpec(memory_space=pltpu.VMEM)
    return pl.pallas_call(
        query_kernel,
        out_shape=jax.ShapeDtypeStruct((HEADS * ROWS, HEAD_K), jnp.bfloat16),
        in_specs=[pl.BlockSpec(memory_space=pltpu.SMEM)] + [vmem] * 2 + [pl.BlockSpec(memory_space=pl.ANY)] * SHARDS,
        out_specs=vmem,
        scratch_shapes=[pltpu.VMEM((D, HEADS * HEAD_K), jnp.bfloat16), pltpu.SemaphoreType.DMA((SHARDS,))],
        compiler_params=pltpu.CompilerParams(vmem_limit_bytes=VMEM_LIMIT),
        cost_estimate=pl.CostEstimate(flops=1_600_000_000, bytes_accessed=4_000_000, transcendentals=0),
        name="query",
    )(order, hidden, angles, *blocks)


def attention_kernel(order, coarse, *refs):
    queries, pairs, blocks = refs[0], refs[1:5], refs[5 : 5 + SHARDS]
    out, weight, sems = refs[5 + SHARDS :]
    copies = load_rows(order, blocks, OUT_AT, 0, D, weight, sems)
    keys = jnp.concatenate([pair[:, :HEAD_K] for pair in pairs], axis=0)
    values = jnp.concatenate([pair[:, HEAD_K:] for pair in pairs], axis=0)
    mixed = []
    for head in range(HEADS):
        query = queries[head * ROWS : (head + 1) * ROWS]
        scores = lax.dot_general(query, keys, (((1,), (1,)), ((), ())), preferred_element_type=jnp.float32)
        scores = scores * HEAD_K ** (-0.5)
        raised = jnp.exp(scores - jnp.max(scores, axis=-1, keepdims=True))
        weights = raised * (1.0 / jnp.sum(raised, axis=-1, keepdims=True))
        mixed.append(dot(weights.astype(jnp.bfloat16), values).astype(jnp.bfloat16)[:, :HEAD_V])
    for copy in copies:
        copy.wait()
    total = coarse[...].astype(jnp.float32)
    for head in range(HEADS):
        total = total + dot(mixed[head], weight[head * HEAD_V : (head + 1) * HEAD_V])
    out[...] = total.astype(jnp.bfloat16)


def attention(order, coarse, query, pairs, blocks):
    vmem = pl.BlockSpec(memory_space=pltpu.VMEM)
    return pl.pallas_call(
        attention_kernel,
        out_shape=jax.ShapeDtypeStruct((ROWS, D), jnp.bfloat16),
        in_specs=[pl.BlockSpec(memory_space=pltpu.SMEM)] + [vmem] * 6 + [pl.BlockSpec(memory_space=pl.ANY)] * SHARDS,
        out_specs=vmem,
        scratch_shapes=[pltpu.VMEM((D, D), jnp.bfloat16), pltpu.SemaphoreType.DMA((SHARDS,))],
        compiler_params=pltpu.CompilerParams(vmem_limit_bytes=VMEM_LIMIT),
        cost_estimate=pl.CostEstimate(flops=3_000_000_000, bytes_accessed=6_000_000, transcendentals=1_000_000),
        name="attention",
    )(order, coarse, query, *pairs, *blocks)


def move(value, pairs):
    return lax.ppermute(value, AXES, pairs)


def body(
    tokens,
    stem_weight,
    stem_bias,
    conv_gain,
    conv_weight,
    conv_bias,
    attn_gain,
    w_query,
    w_key,
    w_value,
    w_out,
):
    seq = lax.axis_index("seq")
    line = tokens.reshape(ROWS, 128)
    own = pack(conv_weight, w_out, w_query, w_key, w_value)
    own_o = move(own, FROM_CORE)
    y = move(own, FROM_Y)
    za = move(own, FROM_Z)
    low = lax.ppermute(line[-1:], "seq", [(i, (i + 1) % 8) for i in range(8)])
    high = lax.ppermute(line[:1], "seq", [(i, (i - 1) % 8) for i in range(8)])
    order = jnp.asarray(PLACES)[lax.axis_index("dp"), seq]
    front, taps, vectors = stem_front(order, line, stem_weight, stem_bias[None], conv_gain[None])
    y, za, own_o, low, high, front = lax.optimization_barrier((y, za, own_o, low, high, front))

    y_o, za_o = move(y, FROM_CORE), move(za, FROM_CORE)
    zb = move(za, FROM_X)
    yza = move(za, FROM_Y)
    zz = move(za, FROM_Z)
    back = stem_back(line, taps, vectors)
    patch = edges(order, line, low, high, taps, vectors)
    rest = (conv_bias[None], attn_gain[None], jnp.asarray(ANGLES)[seq])
    zb, yza, zz, back, patch, *rest = lax.optimization_barrier((zb, yza, zz, back, patch, *rest))
    yzb = move(yza, FROM_X)
    yzz = move(zz, FROM_Y)
    blocks = [own, own_o, y, za, y_o, za_o, zb, zz, yza] + [move(b, FROM_CORE) for b in (zb, zz, yza)]
    total = conv_part(0, order, front, back, patch, blocks)
    yzb, yzz, total = lax.optimization_barrier((yzb, yzz, total))
    blocks += [yzb, yzz, move(yzb, FROM_CORE), move(yzz, FROM_CORE)]
    coarse, hidden, pair = conv_part(1, order, front, back, patch, blocks, (total, *rest))

    near = lax.ppermute(pair, "seq", [(i, i ^ 1) for i in range(8)])
    both = jnp.concatenate([pair, near], axis=0)
    pairs = [both] + [
        lax.ppermute(both, "seq", [(i, (i + shift) % 8) for i in range(8)]) for shift in (2, 6, 4)
    ]
    query = query_of(order, hidden, rest[2], blocks)
    return attention(order, coarse, query, pairs, blocks)[None]


def solution(mesh):
    in_specs = (
        P("dp", "seq"),
        P(),
        P(),
        P(),
        P(None, "dp", None),
        P(),
        P(),
        P("dp", None),
        P("dp", None),
        P("dp", None),
        P("dp", None),
    )
    out_specs = P("dp", "seq", None)
    return jax.shard_map(body, mesh=mesh, in_specs=in_specs, out_specs=out_specs, check_vma=False)
```

```python
import functools

import jax
import jax.numpy as jnp
import numpy as np
from jax import lax
from jax.experimental import pallas as pl
from jax.experimental.pallas import tpu as pltpu
from jax.sharding import PartitionSpec as P

D_STEM = 768
D = 1536
HEADS = 8
HEAD_K = 128
HEAD_V = 192
KW_STEM = 15
KW = 5
POOL_A = 8
POOL_B = 16
SHARDS = 16
CONV_ROWS = D_STEM // SHARDS
PROJ_ROWS = D // SHARDS
OUT_AT = KW * CONV_ROWS
QKV_AT = OUT_AT + PROJ_ROWS
BLOCK_ROWS = QKV_AT + PROJ_ROWS
ROWS = 128
HALO = 24
EPSILON = 1e-06
AXES = ("dp", "seq")
VMEM_LIMIT = 60 * 1024 * 1024


def device_of(x, y, z, core):
    x, y, z = x % 4, y % 4, z % 4
    return ((y % 2) * 8 + z * 2 + core) * 8 + (x * 2 + y // 2)


def received_from(source):
    pairs = []
    for x in range(4):
        for y in range(4):
            for z in range(4):
                for core in range(2):
                    pairs.append((device_of(*source(x, y, z, core)), device_of(x, y, z, core)))
    return sorted(pairs)


def side(core):
    return 1 - 2 * core


def turn(x, core):
    return 1 - 2 * ((x + core) % 2)


FROM_Y = received_from(lambda x, y, z, core: (x, y + side(core), z, core))
FROM_X = received_from(lambda x, y, z, core: (x + side(core), y, z, core))
FROM_Z = received_from(lambda x, y, z, core: (x, y, z + turn(x, core), core))
FROM_Z_CROSS = received_from(lambda x, y, z, core: (x, y, z + turn(x, 1 - core), 1 - core))
FROM_CORE = received_from(lambda x, y, z, core: (x, y, z, 1 - core))


def shard_order():
    orders = np.zeros((SHARDS, 8, SHARDS), np.int32)
    for dp in range(SHARDS):
        for seq in range(8):
            y_low, z, core, x = dp // 8, (dp // 2) % 4, dp % 2, seq // 2

            def names(c):
                turned = turn(x, c)

                def shard(other, dz):
                    return (y_low ^ other) * 8 + (z + dz) % 4 * 2 + c

                return dict(
                    own=shard(0, 0), y=shard(1, 0), za=shard(0, turned), zb=shard(0, -turned),
                    zz=shard(0, 2), yza=shard(1, turned), yzb=shard(1, -turned), yzz=shard(1, 2),
                )

            mine, other = names(core), names(1 - core)
            order = [mine["own"], other["own"], mine["y"], mine["za"], other["y"], other["za"]]
            order += [mine["zb"], mine["zz"], mine["yza"], other["zb"], other["zz"], other["yza"]]
            order += [mine["yzb"], mine["yzz"], other["yzb"], other["yzz"]]
            orders[dp, seq] = order
    return orders


def trig():
    half = HEAD_K // 2
    freqs = np.float32(10000.0) ** (-np.arange(half, dtype=np.float32) / np.float32(half))
    angles = np.arange(8 * ROWS, dtype=np.float32)[:, None] * freqs[None, :]
    cosine, sine = np.cos(angles.astype(np.float64)), np.sin(angles.astype(np.float64))
    table = [np.concatenate([cosine, cosine], axis=1), np.concatenate([-sine, sine], axis=1)]
    return np.stack([t.reshape(8, ROWS, HEAD_K) for t in table], axis=1).astype(np.float32)


PLACES = np.concatenate(
    [shard_order(), np.broadcast_to(np.arange(8, dtype=np.int32)[None, :, None], (SHARDS, 8, 1))], axis=2
)
ANGLES = trig()


def dot(a, b):
    return jnp.dot(a, b, preferred_element_type=jnp.float32)


def gelu(x):
    return jax.nn.gelu(x)


STEM_ROWS = 512
FULL = POOL_B * ROWS


def hits_of(wide, g):
    width = wide.shape[1]
    token = lax.broadcasted_iota(jnp.int32, (width, 128), 0)
    lane = lax.broadcasted_iota(jnp.int32, (width, 128), 1)
    pick = (token == 120 + 8 * g + lane // 4).astype(jnp.float32).astype(jnp.bfloat16)
    spread = dot(wide, pick)
    code = (lax.broadcasted_iota(jnp.int32, spread.shape, 1) % 4 + 1).astype(jnp.float32)
    return (spread == code).astype(jnp.float32)


def strongest(rows, taps, columns):
    most = dot(rows, taps[0:128, columns])
    for offset in range(1, POOL_A):
        most = jnp.maximum(most, dot(rows, taps[offset * 128 : (offset + 1) * 128, columns]))
    return most


def stem_norm(most, bias, gain):
    pooled = gelu(most + bias).astype(jnp.bfloat16).astype(jnp.float32)
    scale = lax.rsqrt(jnp.mean(pooled * pooled, axis=-1, keepdims=True) + EPSILON)
    return pooled * scale * gain


def stem_kernel(order, tokens, weight, bias, gain, out, taps, vectors, hits, best):
    lane = lax.broadcasted_iota(jnp.int32, (D_STEM, D_STEM), 1)
    source = lax.broadcasted_iota(jnp.int32, (1, D_STEM), 1)
    for i in range(SHARDS):
        here = lax.broadcasted_iota(jnp.int32, (1, D_STEM), 1)
        source = jnp.where(here >= i * CONV_ROWS, here + (order[i] - i) * CONV_ROWS, source)
    channel = lax.broadcasted_iota(jnp.int32, (D_STEM, D_STEM), 0)
    chosen = (channel == source).astype(jnp.float32).astype(jnp.bfloat16)
    parts = []
    for vector in (bias[...], gain[...]):
        for _ in range(3):
            parts.append(vector.astype(jnp.bfloat16).astype(jnp.float32))
            vector = vector - parts[-1]
    parts = jnp.concatenate(parts + [jnp.zeros((10, D_STEM), jnp.float32)], axis=0)
    parts = dot(parts.astype(jnp.bfloat16), chosen)
    vectors[0:1] = parts[0:1] + parts[1:2] + parts[2:3]
    vectors[1:2] = parts[3:4] + parts[4:5] + parts[5:6]
    vectors[2:] = jnp.zeros((6, D_STEM), jnp.float32)
    moved = dot(weight[...], chosen).astype(jnp.bfloat16)
    row = lax.broadcasted_iota(jnp.int32, (POOL_A * 128, 4 * KW_STEM), 0)
    tap = lax.broadcasted_iota(jnp.int32, (POOL_A * 128, 4 * KW_STEM), 1)
    place = (row % 128 == tap + 4 * (row // 128 + 1)).astype(jnp.float32).astype(jnp.bfloat16)
    taps[...] = dot(place, moved).astype(jnp.bfloat16)

    stem_rows(0, tokens, taps, vectors, out, hits, best)


def stem_rows(half, tokens, taps, vectors, out, hits, best):
    held = tokens[...].astype(jnp.float32)
    before, after = pltpu.roll(held, 1, 0), pltpu.roll(held, ROWS - 1, 0)
    wide = jnp.concatenate([before, held, after], axis=1).astype(jnp.bfloat16)
    for k in range(POOL_B // 2):
        hits[k * ROWS : (k + 1) * ROWS] = hits_of(wide, half * (POOL_B // 2) + k).astype(jnp.bfloat16)

    def one(i, _):
        rows = hits[pl.ds(pl.multiple_of(i * STEM_ROWS, STEM_ROWS), STEM_ROWS)]
        for n in range(D_STEM // 256):
            here = slice(n * 256, (n + 1) * 256)
            best[:, here] = strongest(rows, taps, here)
        for k in range(STEM_ROWS // ROWS):
            block = stem_norm(best[k * ROWS : (k + 1) * ROWS], vectors[0:1], vectors[1:2])
            out[i * (STEM_ROWS // ROWS) + k + 2 * half] = block.astype(jnp.bfloat16)
        return 0

    lax.fori_loop(0, FULL // 2 // STEM_ROWS, one, 0)
    for i in range(2):
        source, to, by = (i, 8 + i, ROWS - 1) if half == 0 else (8 + i, i, 1)
        out[to] = pltpu.roll(out[source].astype(jnp.float32), by, 0).astype(jnp.bfloat16)


def stem_front(order, tokens, weight, bias, gain):
    vmem = pl.BlockSpec(memory_space=pltpu.VMEM)
    return pl.pallas_call(
        stem_kernel,
        out_shape=(
            jax.ShapeDtypeStruct((POOL_B // 2 + 2, ROWS, D_STEM), jnp.bfloat16),
            jax.ShapeDtypeStruct((POOL_A * 128, D_STEM), jnp.bfloat16),
            jax.ShapeDtypeStruct((8, D_STEM), jnp.float32),
        ),
        in_specs=[pl.BlockSpec(memory_space=pltpu.SMEM)] + [vmem] * 4,
        out_specs=(vmem, vmem, vmem),
        scratch_shapes=[
            pltpu.VMEM((FULL // 2, 128), jnp.bfloat16),
            pltpu.VMEM((STEM_ROWS, D_STEM), jnp.float32),
        ],
        compiler_params=pltpu.CompilerParams(vmem_limit_bytes=VMEM_LIMIT),
        cost_estimate=pl.CostEstimate(flops=4_000_000_000, bytes_accessed=5_000_000, transcendentals=800_000),
        name="stem_front",
    )(order, tokens, weight, bias, gain)


def stem_back(tokens, taps, vectors):
    vmem = pl.BlockSpec(memory_space=pltpu.VMEM)
    return pl.pallas_call(
        functools.partial(stem_rows, 1),
        out_shape=jax.ShapeDtypeStruct((POOL_B // 2 + 2, ROWS, D_STEM), jnp.bfloat16),
        in_specs=[vmem] * 3,
        out_specs=vmem,
        scratch_shapes=[
            pltpu.VMEM((FULL // 2, 128), jnp.bfloat16),
            pltpu.VMEM((STEM_ROWS, D_STEM), jnp.float32),
        ],
        compiler_params=pltpu.CompilerParams(vmem_limit_bytes=VMEM_LIMIT),
        cost_estimate=pl.CostEstimate(flops=3_500_000_000, bytes_accessed=4_000_000, transcendentals=800_000),
        name="stem_back",
    )(tokens, taps, vectors)


def edge_kernel(order, tokens, low_row, high_row, taps, vectors, out):
    at_start = order[SHARDS] == 0
    at_end = order[SHARDS] == 7
    low = jnp.where(at_start, 0, low_row[...])
    high = jnp.where(at_end, 0, high_row[...])
    first, last = tokens[0:1], tokens[ROWS - 1 : ROWS]
    lines = [(low, low, first), (low, first, first), (last, last, high), (last, high, high)]
    wide = jnp.concatenate([jnp.concatenate(line, axis=1) for line in lines] + [jnp.zeros((12, 384), jnp.int32)], axis=0)
    wide = wide.astype(jnp.float32).astype(jnp.bfloat16)
    by_row = {g: hits_of(wide, g) for g in (0, 1, 14, 15)}
    wanted = [(14, 0), (15, 0), (0, 1), (15, 2), (0, 3), (1, 3)]
    rows = [by_row[g][line : line + 1] for g, line in wanted] + [jnp.zeros((10, 128), jnp.float32)]
    rows = jnp.concatenate(rows, axis=0).astype(jnp.bfloat16)
    normed = stem_norm(strongest(rows, taps, slice(0, D_STEM)), vectors[0:1], vectors[1:2])
    row = lax.broadcasted_iota(jnp.int32, normed.shape, 0)
    outside = ((row < 2) & at_start) | ((row > 3) & at_end)
    out[...] = jnp.where(outside, 0.0, normed)


def edges(order, tokens, low, high, taps, vectors):
    vmem = pl.BlockSpec(memory_space=pltpu.VMEM)
    return pl.pallas_call(
        edge_kernel,
        out_shape=jax.ShapeDtypeStruct((16, D_STEM), jnp.float32),
        in_specs=[pl.BlockSpec(memory_space=pltpu.SMEM)] + [vmem] * 5,
        out_specs=vmem,
        compiler_params=pltpu.CompilerParams(vmem_limit_bytes=VMEM_LIMIT),
        cost_estimate=pl.CostEstimate(flops=30_000_000, bytes_accessed=2_000_000, transcendentals=10_000),
        name="edges",
    )(order, tokens, low, high, taps, vectors)


def pack_kernel(conv, w_out, w_query, w_key, w_value, out):
    for tap in range(KW):
        out[tap * CONV_ROWS : (tap + 1) * CONV_ROWS] = conv[tap]
    out[OUT_AT:QKV_AT] = w_out[...]
    at = 0
    for piece in (w_query, w_key, w_value):
        width = piece.shape[1]
        out[QKV_AT:, at : at + width] = piece[...]
        at += width
    out[QKV_AT:, at:] = jnp.zeros((PROJ_ROWS, D - at), jnp.bfloat16)


def pack(*pieces):
    vmem = pl.BlockSpec(memory_space=pltpu.VMEM)
    return pl.pallas_call(
        pack_kernel,
        out_shape=jax.ShapeDtypeStruct((BLOCK_ROWS, D), jnp.bfloat16),
        in_specs=[vmem] * 5,
        out_specs=vmem,
        compiler_params=pltpu.CompilerParams(vmem_limit_bytes=VMEM_LIMIT),
        name="pack",
    )(*pieces)


PARTS = ((0, 512), (512, 256))


def pieces_of(part):
    start, size = PARTS[part]
    pieces = []
    at = start
    while at < start + size:
        block, row = divmod(at, CONV_ROWS)
        rows = min(CONV_ROWS - row, start + size - at)
        pieces.append((block, row, rows, at - start))
        at += rows
    return pieces


TILES = ((512, 8), (256, 8))
KV_WIDTH = 384


def conv_kernel(part, count, order, front, back, patch, *refs):
    blocks, refs = refs[:count], refs[count:]
    if part == 1:
        acc_in, bias, gain, angles = refs[:4]
        coarse, hidden, pair = refs[4:7]
        refs = refs[7:]
    else:
        out, refs = refs[0], refs[1:]
    held, lhs_a, lhs_b, lhs_c, lhs_d, w_a, w_b, w_c, w_d, w_1, sems, held_sems = refs[:12]
    if part == 1:
        most_ref, least_ref, weight, weight_sems = refs[12:]
    pieces = pieces_of(part)
    first = pieces[0][0]
    start, size = PARTS[part]
    tile, pairs = TILES[part]
    third, step = pl.program_id(0), pl.program_id(1)
    columns = pl.ds(pl.multiple_of(third * tile, tile), tile)
    homes = [(w_a, 0), (w_1, 0), (w_d, 0), (w_a, size), (w_d, size)]

    def copies():
        return [
            pltpu.make_async_copy(
                blocks[block - first].at[pl.ds(tap * CONV_ROWS + row, rows)],
                homes[tap][0].at[pl.ds(homes[tap][1] + to, rows)],
                sems.at[tap * len(pieces) + i],
            )
            for tap in range(KW)
            for i, (block, row, rows, to) in enumerate(pieces)
        ]

    def row_copies():
        return [
            pltpu.make_async_copy(
                source.at[pl.ds(at, rows), :, pl.ds(start, size)],
                held.at[pl.ds(to, rows)],
                held_sems.at[i],
            )
            for i, (source, at, rows, to) in enumerate(
                ((front, 0, 8, 2), (back, 0, 2, 0), (back, 2, 8, 10), (front, 8, 2, 18))
            )
        ]

    def projection_copies():
        return [
            pltpu.make_async_copy(
                block.at[pl.ds(QKV_AT, PROJ_ROWS), pl.ds(HEADS * HEAD_K, KV_WIDTH)],
                weight.at[pl.ds(pl.multiple_of(order[(first + i) % SHARDS] * PROJ_ROWS, PROJ_ROWS), PROJ_ROWS)],
                weight_sems.at[i],
            )
            for i, block in enumerate(blocks)
        ]

    @pl.when((third == 0) & (step == 0))
    def _():
        for copy in row_copies() + copies():
            copy.start()
        if part == 1:
            for copy in projection_copies():
                copy.start()
        for copy in row_copies():
            copy.wait()
        row = lax.broadcasted_iota(jnp.int32, (16, size), 0)
        edge = patch[...]
        for i, block in enumerate((0, 1, 2, POOL_B + 1, POOL_B + 2, POOL_B + 3)):
            at, which = (0, 0) if i < 3 else (ROWS - 16, 15)
            old = held[block, at : at + 16].astype(jnp.float32)
            held[block, at : at + 16] = jnp.where(row == which, edge[i : i + 1], old).astype(jnp.bfloat16)
        for m in range(POOL_B // 2):
            even, odd = [held[2 * m + 2 * k] for k in range(3)], [held[2 * m + 2 * k + 1] for k in range(3)]
            lhs_a[m, :, :size] = even[0] - even[1]
            lhs_a[m, :, size:] = odd[1] - even[2]
            lhs_b[m, :, :size] = odd[0] + even[1]
            lhs_b[m, :, size:] = even[2]
            lhs_c[m] = even[1] - odd[0]
            lhs_d[m, :, :size] = odd[0] - odd[1]
            lhs_d[m, :, size:] = even[2] - odd[2]
        for copy in copies():
            copy.wait()

    @pl.when(step == 0)
    def _():
        outer = (w_a[:size, columns].astype(jnp.float32) + w_d[:size, columns].astype(jnp.float32)) * 0.5
        inner = w_1[:, columns].astype(jnp.float32) * 0.5
        w_b[:size] = (outer + inner).astype(jnp.bfloat16)
        w_c[...] = (outer - inner).astype(jnp.bfloat16)
        w_b[size:] = w_a[size:, columns] + w_d[size:, columns]

    def part_of(lhs):
        return lhs[pl.ds(step * pairs, pairs)].reshape(pairs * ROWS, -1)

    a = dot(part_of(lhs_a), w_a[:, columns])
    b = dot(part_of(lhs_b), w_b[...])
    c = dot(part_of(lhs_c), w_c[...])
    d = dot(part_of(lhs_d), w_d[:, columns])
    even = (a + (b + c)).reshape(pairs, ROWS, tile)
    odd = ((b - c) - d).reshape(pairs, ROWS, tile)
    if part == 1:
        even = even + acc_in[0]
        odd = odd + acc_in[1]
    else:
        out[0] = even
        out[1] = odd
        return
    most = jnp.max(jnp.maximum(even, odd), axis=0)
    least = jnp.min(jnp.minimum(even, odd), axis=0)

    @pl.when(step == 0)
    def _():
        most_ref[...] = most
        least_ref[...] = least

    last = POOL_B // 2 // pairs - 1
    for n in range(D // tile):

        @pl.when((step == last) & (third == n))
        def _():
            here = slice(n * tile, (n + 1) * tile)
            shift = bias[:, here]
            high = jnp.maximum(most_ref[...], most) + shift
            low = jnp.minimum(least_ref[...], least) + shift
            coarse[:, here] = jnp.maximum(gelu(high), gelu(low)).astype(jnp.bfloat16)

    @pl.when((step == last) & (third == D // tile - 1))
    def _():
        residual = coarse[...].astype(jnp.float32)
        scale = lax.rsqrt(jnp.mean(residual * residual, axis=-1, keepdims=True) + EPSILON)
        hidden[...] = (residual * scale * gain[...]).astype(jnp.bfloat16)
        for copy in projection_copies():
            copy.wait()
        made = dot(hidden[...], weight[...])
        pair[:, :HEAD_K] = turned(made[:, :HEAD_K], angles[0], angles[1]).astype(jnp.bfloat16)
        pair[:, HEAD_K:] = made[:, HEAD_K:].astype(jnp.bfloat16)


def conv_part(part, order, front, back, patch, blocks, rest=()):
    pieces = pieces_of(part)
    start, size = PARTS[part]
    tile, pairs = TILES[part]
    used = blocks[: pieces[-1][0] + 1] if part == 0 else blocks[pieces[0][0] :] + blocks[: pieces[0][0]]
    args = [order, front, back, patch, *used]
    whole = pl.BlockSpec(memory_space=pltpu.VMEM)
    in_specs = [
        pl.BlockSpec(memory_space=pltpu.SMEM),
        pl.BlockSpec(memory_space=pltpu.HBM),
        pl.BlockSpec(memory_space=pltpu.HBM),
        pl.BlockSpec((16, size), lambda i, j: (0, start // size)),
    ]
    in_specs += [pl.BlockSpec(memory_space=pltpu.HBM)] * len(used)
    acc_spec = pl.BlockSpec((2, pairs, ROWS, tile), lambda i, j: (0, j, 0, i))
    lhs = (POOL_B // 2, ROWS)
    scratch = [
        pltpu.VMEM((POOL_B + 4, ROWS, size), jnp.bfloat16),
        pltpu.VMEM((*lhs, 2 * size), jnp.bfloat16),
        pltpu.VMEM((*lhs, 2 * size), jnp.bfloat16),
        pltpu.VMEM((*lhs, size), jnp.bfloat16),
        pltpu.VMEM((*lhs, 2 * size), jnp.bfloat16),
        pltpu.VMEM((2 * size, D), jnp.bfloat16),
        pltpu.VMEM((2 * size, tile), jnp.bfloat16),
        pltpu.VMEM((size, tile), jnp.bfloat16),
        pltpu.VMEM((2 * size, D), jnp.bfloat16),
        pltpu.VMEM((size, D), jnp.bfloat16),
        pltpu.SemaphoreType.DMA((KW * len(pieces),)),
        pltpu.SemaphoreType.DMA((4,)),
    ]
    if part == 1:
        args += rest
        in_specs += [acc_spec] + [whole] * 3
        out_shape = (
            jax.ShapeDtypeStruct((ROWS, D), jnp.bfloat16),
            jax.ShapeDtypeStruct((ROWS, D), jnp.bfloat16),
            jax.ShapeDtypeStruct((ROWS, KV_WIDTH), jnp.bfloat16),
        )
        out_spec = (whole, whole, whole)
        scratch += [pltpu.VMEM((ROWS, tile), jnp.float32)] * 2
        scratch += [pltpu.VMEM((D, KV_WIDTH), jnp.bfloat16), pltpu.SemaphoreType.DMA((SHARDS,))]
    else:
        out_shape = jax.ShapeDtypeStruct((2, POOL_B // 2, ROWS, D), jnp.float32)
        out_spec = acc_spec
    return pl.pallas_call(
        functools.partial(conv_kernel, part, len(used)),
        grid=(D // tile, POOL_B // 2 // pairs),
        out_shape=out_shape,
        in_specs=in_specs,
        out_specs=out_spec,
        scratch_shapes=scratch,
        compiler_params=pltpu.CompilerParams(vmem_limit_bytes=VMEM_LIMIT),
        cost_estimate=pl.CostEstimate(flops=size * 22_020_096, bytes_accessed=20_000_000, transcendentals=0),
        name="conv",
    )(*args)


def turned(values, cosine, sine):
    return values * cosine + pltpu.roll(values, HEAD_K // 2, 1) * sine


def load_rows(order, blocks, row, column, width, target, sems):
    copies = [
        pltpu.make_async_copy(
            block.at[pl.ds(row, PROJ_ROWS), pl.ds(column, width)],
            target.at[pl.ds(pl.multiple_of(order[i] * PROJ_ROWS, PROJ_ROWS), PROJ_ROWS)],
            sems.at[i],
        )
        for i, block in enumerate(blocks)
    ]
    for copy in copies:
        copy.start()
    return copies


def query_kernel(order, hidden, angles, *refs):
    blocks = refs[:SHARDS]
    out, weight, sems = refs[SHARDS:]
    for copy in load_rows(order, blocks, QKV_AT, 0, HEADS * HEAD_K, weight, sems):
        copy.wait()
    query = dot(hidden[...], weight[...])
    for head in range(HEADS):
        one = query[:, head * HEAD_K : (head + 1) * HEAD_K]
        out[head * ROWS : (head + 1) * ROWS] = turned(one, angles[0], angles[1]).astype(jnp.bfloat16)


def query_of(order, hidden, angles, blocks):
    vmem = pl.BlockSpec(memory_space=pltpu.VMEM)
    return pl.pallas_call(
        query_kernel,
        out_shape=jax.ShapeDtypeStruct((HEADS * ROWS, HEAD_K), jnp.bfloat16),
        in_specs=[pl.BlockSpec(memory_space=pltpu.SMEM)] + [vmem] * 2 + [pl.BlockSpec(memory_space=pltpu.HBM)] * SHARDS,
        out_specs=vmem,
        scratch_shapes=[pltpu.VMEM((D, HEADS * HEAD_K), jnp.bfloat16), pltpu.SemaphoreType.DMA((SHARDS,))],
        compiler_params=pltpu.CompilerParams(vmem_limit_bytes=VMEM_LIMIT),
        cost_estimate=pl.CostEstimate(flops=1_600_000_000, bytes_accessed=4_000_000, transcendentals=0),
        name="query",
    )(order, hidden, angles, *blocks)


def attention_kernel(order, coarse, *refs):
    queries, pairs, blocks = refs[0], refs[1:5], refs[5 : 5 + SHARDS]
    out, weight, sems = refs[5 + SHARDS :]
    copies = load_rows(order, blocks, OUT_AT, 0, D, weight, sems)
    keys = jnp.concatenate([pair[:, :HEAD_K] for pair in pairs], axis=0)
    values = jnp.concatenate([pair[:, HEAD_K:] for pair in pairs], axis=0)
    mixed = []
    for head in range(HEADS):
        query = queries[head * ROWS : (head + 1) * ROWS]
        scores = lax.dot_general(query, keys, (((1,), (1,)), ((), ())), preferred_element_type=jnp.float32)
        scores = scores * HEAD_K ** (-0.5)
        raised = jnp.exp(scores - jnp.max(scores, axis=-1, keepdims=True))
        weights = raised * (1.0 / jnp.sum(raised, axis=-1, keepdims=True))
        mixed.append(dot(weights.astype(jnp.bfloat16), values).astype(jnp.bfloat16)[:, :HEAD_V])
    for copy in copies:
        copy.wait()
    total = coarse[...].astype(jnp.float32)
    for head in range(HEADS):
        total = total + dot(mixed[head], weight[head * HEAD_V : (head + 1) * HEAD_V])
    out[...] = total.astype(jnp.bfloat16)


def attention(order, coarse, query, pairs, blocks):
    vmem = pl.BlockSpec(memory_space=pltpu.VMEM)
    return pl.pallas_call(
        attention_kernel,
        out_shape=jax.ShapeDtypeStruct((ROWS, D), jnp.bfloat16),
        in_specs=[pl.BlockSpec(memory_space=pltpu.SMEM)] + [vmem] * 6 + [pl.BlockSpec(memory_space=pltpu.HBM)] * SHARDS,
        out_specs=vmem,
        scratch_shapes=[pltpu.VMEM((D, D), jnp.bfloat16), pltpu.SemaphoreType.DMA((SHARDS,))],
        compiler_params=pltpu.CompilerParams(vmem_limit_bytes=VMEM_LIMIT),
        cost_estimate=pl.CostEstimate(flops=3_000_000_000, bytes_accessed=6_000_000, transcendentals=1_000_000),
        name="attention",
    )(order, coarse, query, *pairs, *blocks)


def move(value, pairs):
    return lax.ppermute(value, AXES, pairs)


def body(
    tokens,
    stem_weight,
    stem_bias,
    conv_gain,
    conv_weight,
    conv_bias,
    attn_gain,
    w_query,
    w_key,
    w_value,
    w_out,
):
    seq = lax.axis_index("seq")
    line = tokens.reshape(ROWS, 128)
    own = pack(conv_weight, w_out, w_query, w_key, w_value)
    own_o = move(own, FROM_CORE)
    y = move(own, FROM_Y)
    za = move(own, FROM_Z)
    low = lax.ppermute(line[-1:], "seq", [(i, (i + 1) % 8) for i in range(8)])
    high = lax.ppermute(line[:1], "seq", [(i, (i - 1) % 8) for i in range(8)])
    order = jnp.asarray(PLACES)[lax.axis_index("dp"), seq]
    front, taps, vectors = stem_front(order, line, stem_weight, stem_bias[None], conv_gain[None])
    y, za, own_o, low, high, front = lax.optimization_barrier((y, za, own_o, low, high, front))

    y_o, za_o = move(y, FROM_CORE), move(za, FROM_CORE)
    zb = move(za, FROM_X)
    yza = move(za, FROM_Y)
    zz = move(za, FROM_Z)
    back = stem_back(line, taps, vectors)
    patch = edges(order, line, low, high, taps, vectors)
    rest = (conv_bias[None], attn_gain[None], jnp.asarray(ANGLES)[seq])
    zb, yza, zz, back, patch, *rest = lax.optimization_barrier((zb, yza, zz, back, patch, *rest))
    yzb = move(yza, FROM_X)
    yzz = move(zz, FROM_Y)
    yzz_o = move(yza, FROM_Z_CROSS)
    blocks = [own, own_o, y, za, y_o, za_o, zb, zz, yza] + [move(b, FROM_CORE) for b in (zb, zz, yza)]
    total = conv_part(0, order, front, back, patch, blocks)
    yzb, yzz, yzz_o, total = lax.optimization_barrier((yzb, yzz, yzz_o, total))
    blocks += [yzb, yzz, move(yzb, FROM_CORE), yzz_o]
    coarse, hidden, pair = conv_part(1, order, front, back, patch, blocks, (total, *rest))

    near = lax.ppermute(pair, "seq", [(i, i ^ 1) for i in range(8)])
    both = jnp.concatenate([pair, near], axis=0)
    pairs = [both] + [
        lax.ppermute(both, "seq", [(i, (i + shift) % 8) for i in range(8)]) for shift in (2, 6, 4)
    ]
    query = query_of(order, hidden, rest[2], blocks)
    return attention(order, coarse, query, pairs, blocks)[None]


def solution(mesh):
    in_specs = (
        P("dp", "seq"),
        P(),
        P(),
        P(),
        P(None, "dp", None),
        P(),
        P(),
        P("dp", None),
        P("dp", None),
        P("dp", None),
        P("dp", None),
    )
    out_specs = P("dp", "seq", None)
    return jax.shard_map(body, mesh=mesh, in_specs=in_specs, out_specs=out_specs, check_vma=False)
```
